32 devices in a mesh: row: 8 (over y, x, core), col: 4 (over z).
Axes of the slice: x: 2, y: 2, z: 4, core: 2. Of those that a mesh axis runs over, the one named last changes fastest.
Arguments:
- op_tiles: float32 [256, 4, 64, 64], P('row', 'col'), may hold values from -18 to 18
- op_rows: int32 [256, 4], P('row', 'col'), may hold values from 0 to 7
- op_cols: int32 [256, 4], P('row', 'col'), may hold values from 0 to 15
- op_count: int32 [8, 4], P('row', 'col'), may hold values from 1 to 32, as said below
- pro_tiles: float32 [64, 4, 64, 64], P('row', 'col'), may hold values from -0.1875 to 0.1875
- pro_cols: int32 [64, 4], P('row', 'col'), may hold values from 0 to 3
- pro_live: int32 [64, 4], P('row', 'col'), may hold values 0 or 1
Outputs:
- product: float32 [64, 16, 64, 64], P('row', 'col')
- coarse: float32 [16, 16, 64, 64], P('row', 'col')
The draws below stay inside these ranges and needn't reach their ends.
Inputs may be any that keep to these rules, and one draw needn't show every extreme that they name: `op_count`: live slots of each device's list; some device's list is full in every draw.
All inputs are finite; a program needn't handle non-finite values. No bound on the sum of `pro_live` on one device may be relied on, other than what follows from the above.
Results may differ from the reference program's by a relative error of at most 0.0003.
Values sent between devices are 32-bit elements; how exact they have to be, the bound alone decides.
No kernel may reach another device: no remote copies, remote signals or barrier semaphores. Data moves between devices by JAX's collectives and lax.ppermute only.
A program may use at most 128 MiB of HBM per device.

```python
import jax
import jax.numpy as jnp
from jax import lax

TILE = 64
FR = 8
LA = 32
NF = 64
FC = 16
NC = 16
NCC = 4
N_ROW = 8
N_COL = 4


def draw_op_count(key, part):
    base_key, heavy_key, chosen_key = jax.random.split(key, 3)
    light_counts = jax.random.randint(base_key, (N_ROW, N_COL), 1, LA // 2 + 1)
    heavy_marks = jax.random.randint(heavy_key, (N_ROW, N_COL), 0, 8) == 0
    counts = jnp.where(heavy_marks, LA, light_counts).reshape(-1)
    chosen_slot = jax.random.randint(chosen_key, (), 0, N_ROW * N_COL)
    flat_counts = jnp.where(jnp.arange(N_ROW * N_COL) == chosen_slot, LA, counts)
    return flat_counts.reshape(N_ROW, N_COL).astype(jnp.int32)


def touch_ends(entries, own_key, low, top_value):
    longest = entries.shape.index(max(entries.shape))
    spots = []
    for shift in (0, 1):
        where = [jax.random.randint(jax.random.fold_in(own_key, axis), (), 0, length) for axis, length in enumerate(entries.shape)]
        where[longest] = (where[longest] + shift) % entries.shape[longest]
        spots.append(tuple(where))
    return entries.at[spots[0]].set(low).at[spots[1]].set(top_value)


def block_levels(key, extent, cuts, smallest, largest):
    factor_of, own = 1.0, jax.random.fold_in(key, 6)
    for axis_at, blocks in cuts:
        steps = jnp.exp(jax.random.uniform(jax.random.fold_in(own, axis_at), (blocks,), jnp.float32, smallest / len(cuts), largest / len(cuts)))
        factor_of = factor_of * jnp.repeat(steps, extent[axis_at] // blocks).reshape([-1 if axis == axis_at else 1 for axis in range(len(extent))])
    return factor_of


def scatter_about(stream_key, shape, scale, bound, cuts=(), held_as=jnp.bfloat16):
    values = scale * jax.random.normal(stream_key, shape, jnp.float32)
    if cuts:
        values = values * block_levels(stream_key, shape, cuts, -0.22, 0.18)
    return jnp.clip(values, -bound, bound).astype(held_as)


def setup_inputs(seed: int = 0) -> dict:
    keys = jax.random.split(jax.random.key(seed), 8)
    op_tiles = scatter_about(keys[0], (N_ROW * LA, N_COL, TILE, TILE), 3.0, 18.0, ((0, 8), (1, 4)), jnp.float32)
    op_rows = touch_ends(jax.random.randint(keys[1], (N_ROW * LA, N_COL), 0, FR), jax.random.fold_in(keys[1], 1), 0, FR - 1).astype(jnp.int32)
    op_cols = touch_ends(jax.random.randint(keys[2], (N_ROW * LA, N_COL), 0, FC), jax.random.fold_in(keys[2], 1), 0, FC - 1).astype(jnp.int32)
    op_count = draw_op_count(jax.random.fold_in(keys[7], 71), 0)
    pro_tiles = scatter_about(keys[4], (NF, N_COL, TILE, TILE), (TILE * NF // 4) ** -0.5, 0.1875, ((0, 8), (1, 4)), jnp.float32)
    pro_cols = touch_ends(jax.random.randint(keys[5], (NF, N_COL), 0, NCC), jax.random.fold_in(keys[5], 1), 0, NCC - 1).astype(jnp.int32)
    pro_live = touch_ends((jax.random.randint(keys[6], (NF, N_COL), 0, 2) < 1).astype(jnp.int32), jax.random.fold_in(keys[6], 1), 0, 1)
    return {"op_tiles": op_tiles, "op_rows": op_rows, "op_cols": op_cols, "op_count": op_count, "pro_tiles": pro_tiles, "pro_cols": pro_cols, "pro_live": pro_live}


precise = lax.Precision.HIGHEST


def reference(op_tiles, op_rows, op_cols, op_count, pro_tiles, pro_cols, pro_live):
    slot_ids = jnp.arange(LA, dtype=jnp.int32)
    live_op = (slot_ids[None, :, None] < op_count[:, None, :]).astype(jnp.float32)
    row_base = (jnp.arange(N_ROW, dtype=jnp.int32) * FR)[:, None, None]
    col_base = (jnp.arange(N_COL, dtype=jnp.int32) * FC)[None, None, :]
    glob_rows = (op_rows.reshape(N_ROW, LA, N_COL) + row_base).reshape(-1).astype(jnp.int32)
    glob_cols = (op_cols.reshape(N_ROW, LA, N_COL) + col_base).reshape(-1).astype(jnp.int32)
    masked_op = (op_tiles.reshape(N_ROW, LA, N_COL, TILE, TILE) * live_op[..., None, None]).reshape(-1, TILE, TILE)
    masked_pro = pro_tiles * pro_live.astype(jnp.float32)[..., None, None]
    coarse_ids = (pro_cols + (jnp.arange(N_COL, dtype=jnp.int32) * NCC)[None, :]).astype(jnp.int32)
    per_block = LA * N_COL

    def add_block(product_acc, block_id):
        begin_at = (block_id * per_block).astype(jnp.int32)
        tiles_blk = lax.dynamic_slice_in_dim(masked_op, begin_at, per_block, 0)
        rows_blk = lax.dynamic_slice_in_dim(glob_rows, begin_at, per_block, 0)
        cols_blk = lax.dynamic_slice_in_dim(glob_cols, begin_at, per_block, 0)
        right_tiles = masked_pro[cols_blk]
        targets = coarse_ids[cols_blk]
        tile_prods = jnp.einsum("nab,nsbc->nsac", tiles_blk, right_tiles, precision=precise)
        return product_acc.at[rows_blk[:, None], targets].add(tile_prods), None

    product = jnp.zeros((NF, NC, TILE, TILE), jnp.float32)
    product, unused_a = lax.scan(add_block, product, jnp.arange(N_ROW, dtype=jnp.int32))

    def add_coarse(coarse_acc, block_id):
        begin_at = (block_id * FR).astype(jnp.int32)
        left_tiles = lax.dynamic_slice_in_dim(masked_pro, begin_at, FR, 0)
        left_ids = lax.dynamic_slice_in_dim(coarse_ids, begin_at, FR, 0)
        right_rows = lax.dynamic_slice_in_dim(product, begin_at, FR, 0)
        tile_prods = jnp.einsum("ksba,kjbc->ksjac", left_tiles, right_rows, precision=precise)
        return coarse_acc.at[left_ids.reshape(-1)].add(tile_prods.reshape(-1, NC, TILE, TILE)), None

    coarse = jnp.zeros((NC, NC, TILE, TILE), jnp.float32)
    coarse, unused_b = lax.scan(add_coarse, coarse, jnp.arange(N_ROW, dtype=jnp.int32))
    return (product, coarse)
```

```python
import functools

import jax
import jax.numpy as jnp
from jax import lax
from jax.experimental import pallas as pl
from jax.experimental.pallas import tpu as pltpu
from jax.sharding import PartitionSpec as P

COARSEN = 4
GROUP = 16
META = 8
VMEM_BYTES = 48 * 2**20

f32, bf16, i32 = jnp.float32, jnp.bfloat16, jnp.int32
VMEM = pl.BlockSpec(memory_space=pltpu.VMEM)
SMEM = pl.BlockSpec(memory_space=pltpu.SMEM)


def call(kernel, out_shape, n_in, scratch=(), flops=0, nbytes=0):
    return pl.pallas_call(
        kernel,
        out_shape=out_shape,
        in_specs=[VMEM] * n_in,
        out_specs=jax.tree.map(lambda _: VMEM, out_shape),
        scratch_shapes=list(scratch),
        compiler_params=pltpu.CompilerParams(vmem_limit_bytes=VMEM_BYTES),
        cost_estimate=pl.CostEstimate(flops=flops, bytes_accessed=nbytes, transcendentals=0),
    )


def shape(*dims, dtype=f32):
    return jax.ShapeDtypeStruct(dims, dtype)


def pack(fine_cols, coarse_cols, op, pro, rows, cols, count, pro_cols, pro_live, z_pay, r_pay):
    list_len, tile = op.shape[0], op.shape[2]
    fine_rows = pro.shape[0]
    half, quarter = GROUP // 2, fine_rows // 2
    col_index = lax.axis_index("col")
    for block in range(list_len // 2):
        low = block // half * GROUP + block % half
        z_pay[block * tile : (block + 1) * tile, :] = jnp.concatenate([op[low, 0], op[low + half, 0]], axis=1)
    base = list_len // 2 * tile
    for k in range(quarter):
        pair = jnp.concatenate([pro[k, 0], pro[k + quarter, 0]], axis=1)
        r_pay[k * tile : (k + 1) * tile, :] = pair
        turned = pair.T
        z_pay[base + k * tile : base + (k + 1) * tile, :] = jnp.concatenate([turned[:tile], turned[tile:]], axis=1)
    meta = base + quarter * tile
    z_pay[meta : meta + META, :] = jnp.zeros((META, 2 * tile), f32)
    r_pay[quarter * tile : quarter * tile + META, :] = jnp.zeros((META, 2 * tile), f32)
    z_pay[meta : meta + 1, 0:list_len] = rows[...].astype(f32)
    z_pay[meta + 1 : meta + 2, 0:list_len] = (cols[...] + col_index * fine_cols).astype(f32)
    z_pay[meta + 2 : meta + 3, 0:1] = count[...].astype(f32)
    z_pay[meta + 2 : meta + 3, 1:2] = jnp.full((1, 1), col_index, i32).astype(f32)
    live = pro_live[...] > 0
    z_pay[meta + 3 : meta + 4, 0:fine_rows] = jnp.where(live, pro_cols[...] + col_index * coarse_cols, -1).astype(f32)
    r_pay[quarter * tile : quarter * tile + 1, 0:fine_rows] = jnp.where(live, pro_cols[...], -1).astype(f32)


def split(x):
    high = x.astype(bf16)
    return high, (x - high.astype(f32)).astype(bf16)


def halves(pair):
    tile = pair.shape[0]
    high = pair.astype(bf16).astype(f32)
    low = pair - high
    left = lax.broadcasted_iota(i32, pair.shape, 1) < tile
    first = jnp.where(left, high, pltpu.roll(low, tile, 1))
    second = jnp.where(left, pltpu.roll(high, tile, 1), low)
    return first.astype(bf16), second.astype(bf16)


def to_smem(refs, at, dst, sems):
    copies = [
        pltpu.make_async_copy(ref.at[pl.ds(row, META)], dst.at[i], sems.at[i])
        for i, (ref, row) in enumerate(zip(refs, at))
    ]
    for copy in copies:
        copy.start()
    for copy in copies:
        copy.wait()


def add_products(z_pay, meta, panel, target_of, fine_total, coarse_cols, acc, tile, list_len):
    count = meta[2, 0].astype(i32)
    half = GROUP // 2
    for group in range(list_len // GROUP):

        @pl.when(count > group * GROUP)
        def _():
            for p in range(half):
                block = group * half + p
                high, low = split(z_pay[block * tile : (block + 1) * tile, :])
                left = jnp.concatenate([high, low], axis=0)
                rights, places = [], []
                for slot in (group * GROUP + p, group * GROUP + p + half):
                    fine = meta[1, slot].astype(i32)
                    target = target_of(fine)
                    live = jnp.logical_and(slot < count, target >= 0)
                    rights.append(panel[jnp.where(live, fine, fine_total)])
                    places.append(jnp.where(live, meta[0, slot].astype(i32) * coarse_cols + target, 0))
                empty = jnp.zeros_like(rights[0])
                right = jnp.concatenate(
                    [jnp.concatenate([rights[0], empty], axis=0), jnp.concatenate([empty, rights[1]], axis=0)], axis=1
                )
                prods = jnp.dot(left, right, preferred_element_type=f32)
                for side, place in enumerate(places):
                    part = prods[:, side * 2 * tile : (side + 1) * 2 * tile]
                    acc[place] += part[:tile] + part[tile:]


def target_reader(panel_meta, fine_rows, row_count):
    row_index = lax.axis_index("row")

    def target_of(fine):
        return panel_meta[(fine // fine_rows) ^ row_index, 0, fine % fine_rows].astype(i32)

    return target_of


def first_products(n_panel, n_pays, sizes, *refs):
    tile, list_len, fine_rows, coarse_cols = sizes
    r_pays, refs = refs[:n_panel], refs[n_panel:]
    z_pays, refs = refs[:n_pays], refs[n_pays:]
    acc, panel, panel_meta, z_meta, sems = refs
    quarter = fine_rows // 2
    fine_total = fine_rows * n_panel
    row_index = lax.axis_index("row")
    z_at = z_pays[0].shape[0] - META
    to_smem(r_pays, [quarter * tile] * n_panel, panel_meta, sems)
    to_smem(z_pays, [z_at] * n_pays, z_meta, sems)
    acc[...] = jnp.zeros_like(acc)
    panel[fine_total] = jnp.zeros((tile, 2 * tile), bf16)
    for m, r_pay in enumerate(r_pays):
        base = (row_index ^ m) * fine_rows
        for k in range(quarter):
            panel[base + k], panel[base + k + quarter] = halves(r_pay[k * tile : (k + 1) * tile, :])
    target_of = target_reader(panel_meta, fine_rows, n_panel)
    for i, z_pay in enumerate(z_pays):
        add_products(z_pay, z_meta.at[i], panel, target_of, fine_total, coarse_cols, acc, tile, list_len)


def last_products(n_panel, n_pays, n_more, sizes, *refs):
    tile, list_len, fine_rows, coarse_cols = sizes
    acc_in, panel, refs = refs[0], refs[1], refs[2:]
    r_metas, refs = refs[:n_panel], refs[n_panel:]
    z_pays, refs = refs[:n_pays], refs[n_pays:]
    product, keep, send = refs[:3]
    acc, weights, strips, panel_meta, z_meta, sems = refs[3:]
    quarter = fine_rows // 2
    fine_total = fine_rows * n_panel
    row_index = lax.axis_index("row")
    z_at = z_pays[0].shape[0] - META
    to_smem(r_metas, [quarter * tile] * n_panel, panel_meta, sems)
    to_smem(z_pays, [z_at] * n_pays, z_meta, sems)
    acc[...] = acc_in[...]
    target_of = target_reader(panel_meta, fine_rows, n_panel)
    base = list_len // 2 * tile
    n_cols = weights.shape[1] // tile
    for i, z_pay in enumerate(z_pays):
        if i >= n_pays - n_more:
            add_products(z_pay, z_meta.at[i], panel, target_of, fine_total, coarse_cols, acc, tile, list_len)

        @pl.when(z_meta[i, 2, 0] > 0)
        def _(i=i, z_pay=z_pay):
            at = pl.multiple_of(z_meta[i, 2, 1].astype(i32) * tile, tile)
            for k in range(quarter):
                pair = halves(z_pay[base + k * tile : base + (k + 1) * tile, :])
                for kk, wide in zip((k, k + quarter), pair):
                    weights[kk, pl.ds(at, tile), :] = wide

    keep[...] = jnp.zeros_like(keep)
    send[...] = jnp.zeros_like(send)
    for k in range(fine_rows):
        sums = []
        for m in range(coarse_cols):
            part = acc[k * coarse_cols + m]
            total = part + pltpu.roll(part, tile, 1)
            product[k, m] = total[:, :tile]
            sums.append(total)
        left = lax.broadcasted_iota(i32, sums[0].shape, 1) < tile
        strip = jnp.concatenate(
            [jnp.where(left, sums[m], sums[m + 1]) for m in range(0, coarse_cols, 2)], axis=1
        )
        high, low = split(strip)
        right = jnp.concatenate([high, high, low, low], axis=0)
        wide = weights[k]
        strips[k] = jnp.dot(jnp.concatenate([wide, wide], axis=1), right, preferred_element_type=f32)
    owned = keep.shape[1]
    n_chips = keep.shape[0]
    for i, z_pay in enumerate(z_pays):

        @pl.when(z_meta[i, 2, 0] > 0)
        def _(i=i):
            at = pl.multiple_of(z_meta[i, 2, 1].astype(i32) * tile, tile)
            for k in range(fine_rows):
                goal = z_meta[i, 3, k].astype(i32)
                owner = (goal // owned) ^ row_index
                where = (owner // 2, goal % owned)
                live = goal >= 0

                @pl.when(jnp.logical_and(live, owner % 2 == 0))
                def _():
                    keep[where] += strips[k, pl.ds(at, tile), :]

                @pl.when(jnp.logical_and(live, owner % 2 == 1))
                def _():
                    send[where] += strips[k, pl.ds(at, tile), :]


def add_pair(keep, received, *outs):
    for m, out in enumerate(outs):
        out[...] = keep[m] + received[m]


def add_all(*refs):
    *parts, out = refs
    total = parts[0][...]
    for part in parts[1:]:
        total = total + part[...]
    tile = out.shape[2]
    for j in range(out.shape[0]):
        for m in range(out.shape[1]):
            out[j, m] = total[j, :, m * tile : (m + 1) * tile]


def swap(x, axis, mask):
    n = lax.axis_size(axis)
    return lax.ppermute(x, axis, [(i, i ^ mask) for i in range(n)])


def line_gather(own):
    n = lax.axis_size("col")

    def hop(x, first, step):
        pairs = []
        for i in range(first, n - 1, 2):
            if i - (step - 1) >= 0:
                pairs.append((i, i + 1))
            if i + step <= n - 1:
                pairs.append((i + 1, i))
        return lax.ppermute(x, "col", pairs) if pairs else None

    steps, even, odd = [], own, own
    for step in range(1, n):
        even, odd = (
            None if odd is None and step > 1 else hop(own if step == 1 else odd, 0, step),
            None if even is None and step > 1 else hop(own if step == 1 else even, 1, step),
        )
        steps.append([x for x in (even, odd) if x is not None])
    return steps


def shards(op_tiles, op_rows, op_cols, op_count, pro_tiles, pro_cols, pro_live):
    list_len, tile = op_tiles.shape[0], op_tiles.shape[2]
    fine_rows = pro_tiles.shape[0]
    row_count, col_count = lax.axis_size("row"), lax.axis_size("col")
    fine_total = fine_rows * row_count
    fine_cols = fine_total // col_count
    coarse_total = fine_total // COARSEN
    coarse_cols = coarse_total // col_count
    owned = coarse_total // row_count
    n_chips = row_count // 2
    sizes = (tile, list_len, fine_rows, coarse_cols)
    z_rows = (list_len // 2 + fine_rows // 2) * tile + META
    r_rows = fine_rows // 2 * tile + META

    z_pay, r_pay = call(
        functools.partial(pack, fine_cols, coarse_cols),
        (shape(z_rows, 2 * tile), shape(r_rows, 2 * tile)),
        7,
        nbytes=4 * 2**20,
    )(
        op_tiles,
        pro_tiles,
        op_rows.reshape(1, -1),
        op_cols.reshape(1, -1),
        op_count,
        pro_cols.reshape(1, -1),
        pro_live.reshape(1, -1),
    )

    steps = line_gather(z_pay)
    chips = [r_pay] + [swap(r_pay, "row", m) for m in range(2, row_count, 2)]
    cores = [swap(x, "row", 1) for x in chips]
    panel_pays = [x for pair in zip(chips, cores) for x in pair]

    first = [z_pay] + steps[0]
    more = [x for step in steps[1:] for x in step]
    n_first, n_more = len(first), len(more)
    acc, panel = call(
        functools.partial(first_products, row_count, n_first, sizes),
        (shape(fine_rows * coarse_cols, tile, 2 * tile), shape(fine_total + 1, tile, 2 * tile, dtype=bf16)),
        row_count + n_first,
        (
            pltpu.SMEM((row_count, META, 2 * tile), f32),
            pltpu.SMEM((n_first, META, 2 * tile), f32),
            pltpu.SemaphoreType.DMA((max(row_count, n_first),)),
        ),
        flops=2**28,
        nbytes=4 * 2**20,
    )(*panel_pays, *first)

    n_pays = n_first + n_more
    product, keep, send = call(
        functools.partial(last_products, row_count, n_pays, n_more, sizes),
        (
            shape(fine_rows, coarse_cols, tile, tile),
            shape(n_chips, owned, tile, coarse_cols * tile),
            shape(n_chips, owned, tile, coarse_cols * tile),
        ),
        2 + row_count + n_pays,
        (
            pltpu.VMEM((fine_rows * coarse_cols, tile, 2 * tile), f32),
            pltpu.VMEM((fine_rows, col_count * tile, 2 * tile), bf16),
            pltpu.VMEM((fine_rows, col_count * tile, coarse_cols * tile), f32),
            pltpu.SMEM((row_count, META, 2 * tile), f32),
            pltpu.SMEM((n_pays, META, 2 * tile), f32),
            pltpu.SemaphoreType.DMA((max(row_count, n_pays),)),
        ),
        flops=2**28,
        nbytes=4 * 2**20,
    )(acc, panel, *panel_pays, *first, *more)

    received = swap(send, "row", 1)
    part = shape(owned, tile, coarse_cols * tile)
    parts = call(add_pair, (part,) * n_chips, 2, nbytes=2**20)(keep, received)
    others = [swap(parts[m], "row", 2 * m) for m in range(1, n_chips)]
    coarse = call(add_all, shape(owned, coarse_cols, tile, tile), n_chips, nbytes=2**20)(parts[0], *others)
    return (product, coarse)


def solution(mesh):
    return jax.shard_map(
        shards,
        mesh=mesh,
        in_specs=(
            P("row", "col", None, None),
            P("row", "col"),
            P("row", "col"),
            P("row", "col"),
            P("row", "col", None, None),
            P("row", "col"),
            P("row", "col"),
        ),
        out_specs=(P("row", "col", None, None), P("row", "col", None, None)),
        check_vma=False,
    )
```

```python
import functools

import jax
import jax.numpy as jnp
from jax import lax
from jax.experimental import pallas as pl
from jax.experimental.pallas import tpu as pltpu
from jax.sharding import PartitionSpec as P

COARSEN = 4
GROUP = 16
META = 8
VMEM_BYTES = 48 * 2**20
FULL_BYTES = 63 * 2**20

f32, bf16, i32 = jnp.float32, jnp.bfloat16, jnp.int32
VMEM = pl.BlockSpec(memory_space=pltpu.VMEM)
HBM = pl.BlockSpec(memory_space=pltpu.HBM)


def call(kernel, out_shape, n_in, scratch=(), flops=0, nbytes=0, space=VMEM, limit=VMEM_BYTES):
    return pl.pallas_call(
        kernel,
        out_shape=out_shape,
        in_specs=[space] * n_in,
        out_specs=jax.tree.map(lambda _: VMEM, out_shape),
        scratch_shapes=list(scratch),
        compiler_params=pltpu.CompilerParams(vmem_limit_bytes=limit),
        cost_estimate=pl.CostEstimate(flops=flops, bytes_accessed=nbytes, transcendentals=0),
    )


def shape(*dims, dtype=f32):
    return jax.ShapeDtypeStruct(dims, dtype)


def divide(x, n):
    if n & (n - 1):
        return x // n, x % n
    return lax.shift_right_logical(x, n.bit_length() - 1), x & (n - 1)


def pack(fine_cols, coarse_cols, op, pro, rows, cols, count, pro_cols, pro_live, z_pay, r_pay, *scratch):
    sems = scratch[-1]
    sources = (pro, rows, cols, count, pro_cols, pro_live, op.at[pl.ds(0, GROUP)], op.at[pl.ds(GROUP, op.shape[0] - GROUP)])
    copies = [pltpu.make_async_copy(src, dst, sems.at[i]) for i, (src, dst) in enumerate(zip(sources, scratch))]
    for copy in copies:
        copy.start()
    for copy in copies[:-2]:
        copy.wait()
    pro, rows, cols, count, pro_cols, pro_live, low_tiles, high_tiles = scratch[:-1]
    list_len, tile = op.shape[0], op.shape[2]
    fine_rows = pro.shape[0]
    half, quarter = GROUP // 2, fine_rows // 2
    col_index = lax.axis_index("col")
    base = half * tile
    for k in range(quarter):
        pair = jnp.concatenate([pro[k, 0], pro[k + quarter, 0]], axis=1)
        r_pay[k * tile : (k + 1) * tile, :] = pair
        turned = pair.T
        z_pay[base + k * tile : base + (k + 1) * tile, :] = jnp.concatenate([turned[:tile], turned[tile:]], axis=1)
    meta = base + quarter * tile
    high_at = meta + META
    z_pay[meta : meta + META, :] = jnp.zeros((META, 2 * tile), f32)
    r_pay[quarter * tile : quarter * tile + META, :] = jnp.zeros((META, 2 * tile), f32)
    z_pay[meta : meta + 1, 0:list_len] = rows[...].astype(f32)
    z_pay[meta + 1 : meta + 2, 0:list_len] = (cols[...] + col_index * fine_cols).astype(f32)
    z_pay[meta + 2 : meta + 3, 0:1] = count[...].astype(f32)
    z_pay[meta + 2 : meta + 3, 1:2] = jnp.full((1, 1), col_index, i32).astype(f32)
    live = pro_live[...] > 0
    z_pay[meta + 3 : meta + 4, 0:fine_rows] = jnp.where(live, pro_cols[...] + col_index * coarse_cols, -1).astype(f32)
    r_pay[quarter * tile : quarter * tile + 1, 0:fine_rows] = jnp.where(live, pro_cols[...], -1).astype(f32)
    copies[-2].wait()
    for block in range(half):
        z_pay[block * tile : (block + 1) * tile, :] = jnp.concatenate([low_tiles[block, 0], low_tiles[block + half, 0]], axis=1)
    copies[-1].wait()
    for block in range((list_len - GROUP) // 2):
        slot = block // half * GROUP + block % half
        z_pay[high_at + block * tile : high_at + (block + 1) * tile, :] = jnp.concatenate([high_tiles[slot, 0], high_tiles[slot + half, 0]], axis=1)


def split(x):
    high = x.astype(bf16)
    return high, (x - high.astype(f32)).astype(bf16)


def halves(pair):
    tile = pair.shape[0]
    high = pair.astype(bf16).astype(f32)
    low = pair - high
    left = lax.broadcasted_iota(i32, pair.shape, 1) < tile
    first = jnp.where(left, high, pltpu.roll(low, tile, 1))
    second = jnp.where(left, pltpu.roll(high, tile, 1), low)
    return first.astype(bf16), second.astype(bf16)


def add_products(blocks, high_at, groups, meta, ids, panel, sizes, acc):
    tile, list_len, fine_rows, coarse_cols, fine_total, owned = sizes
    count = meta[2, 0].astype(i32)
    half = GROUP // 2
    row_index = lax.axis_index("row")
    for group in groups:

        @pl.when(count > group * GROUP)
        def _(group=group):
            for p in range(half):
                at = p * tile + (high_at + (group - 1) * half * tile if group else 0)
                high, low = split(blocks[at : at + tile, :])
                left = jnp.concatenate([high, low], axis=0)
                rights, places = [], []
                for slot in (group * GROUP + p, group * GROUP + p + half):
                    fine = meta[1, slot].astype(i32)
                    shard, within = divide(fine, fine_rows)
                    target = ids[shard ^ row_index, 0, within].astype(i32)
                    live = jnp.logical_and(slot < count, target >= 0)
                    rights.append(panel[jnp.where(live, fine, fine_total)])
                    places.append(jnp.where(live, meta[0, slot].astype(i32) * coarse_cols + target, 0))
                empty = jnp.zeros_like(rights[0])
                right = jnp.concatenate(
                    [jnp.concatenate([rights[0], empty], axis=0), jnp.concatenate([empty, rights[1]], axis=0)], axis=1
                )
                prods = jnp.dot(left, right, preferred_element_type=f32)
                for side, place in enumerate(places):
                    part = prods[:, side * 2 * tile : (side + 1) * 2 * tile]
                    acc[place] += part[:tile] + part[tile:]


def products(first, last, n_panel, n_prev, n_new, sizes, *refs):
    tile, list_len, fine_rows, coarse_cols, fine_total, owned = sizes
    refs = list(refs)
    take = lambda n: [refs.pop(0) for _ in range(n)]
    if first:
        r_pays = take(n_panel)
    else:
        acc_in, panel, weights_in, ids_in, metas_in = take(5)
    pays = take(n_new)
    if last:
        strips, keep, send = take(3)
        acc, weights, part, goals = take(4)
    elif first:
        acc, weights, metas_out, panel, ids_out = take(5)
    else:
        acc, weights, metas_out = take(3)
    ids, metas, sems = take(3)
    half, quarter = GROUP // 2, fine_rows // 2
    n_all = n_prev + n_new
    row_index = lax.axis_index("row")
    meta_at = (half + quarter) * tile

    moves = [(pay.at[pl.ds(meta_at, META)], metas.at[n_prev + i]) for i, pay in enumerate(pays)]
    if first:
        moves += [(pay.at[pl.ds(quarter * tile, META)], ids.at[m]) for m, pay in enumerate(r_pays)]
    else:
        moves += [(ids_in, ids), (metas_in, metas.at[pl.ds(0, n_prev)])]
    copies = [pltpu.make_async_copy(src, dst, sems.at[i]) for i, (src, dst) in enumerate(moves)]
    for copy in copies:
        copy.start()
    if first:
        acc[...] = jnp.zeros_like(acc)
        panel[fine_total] = jnp.zeros((tile, 2 * tile), bf16)
        for m, pay in enumerate(r_pays):
            at = (row_index ^ m) * fine_rows
            for k in range(quarter):
                panel[at + k], panel[at + k + quarter] = halves(pay[k * tile : (k + 1) * tile, :])
            ids_out[m] = pay[quarter * tile : quarter * tile + META, :]
    else:
        acc[...] = acc_in[...]
        weights[...] = weights_in[...]
    if not last:
        if n_prev:
            metas_out[:n_prev] = metas_in[...]
        for i, pay in enumerate(pays):
            metas_out[n_prev + i] = pay[meta_at : meta_at + META, :]
    for copy in copies:
        copy.wait()

    for i, pay in enumerate(pays):
        meta = metas.at[n_prev + i]

        @pl.when(meta[2, 0] > 0)
        def _(pay=pay, meta=meta):
            at = pl.multiple_of(meta[2, 1].astype(i32) * tile, tile)
            for k in range(quarter):
                block = half + k
                for kk, wide in zip((k, k + quarter), halves(pay[block * tile : (block + 1) * tile, :])):
                    weights[kk, pl.ds(at, tile), :] = wide

        groups = range(list_len // GROUP if pay.shape[0] > meta_at + META else 1)
        add_products(pay, meta_at + META, groups, meta, ids, panel, sizes, acc)
    if not last:
        return

    dump = part.shape[0] - 1
    n_chips = keep.shape[0] // owned
    for i in range(n_all):

        @pl.when(metas[i, 2, 0] > 0)
        def _(i=i):
            source = metas[i, 2, 1].astype(i32)
            for k in range(fine_rows):
                goal = metas[i, 3, k].astype(i32)
                owner, within = divide(jnp.maximum(goal, 0), owned)
                chip, core = divide(owner ^ row_index, 2)
                goals[source, k] = jnp.where(goal >= 0, (core * n_chips + chip) * owned + within, dump)

    part[...] = jnp.zeros_like(part)
    n_sources = weights.shape[1] // tile
    for k in range(fine_rows):
        sums = []
        for m in range(coarse_cols):
            both = acc[k * coarse_cols + m]
            sums.append(both + pltpu.roll(both, tile, 1))
        left = lax.broadcasted_iota(i32, sums[0].shape, 1) < tile
        strip = jnp.concatenate(
            [jnp.where(left, sums[m], sums[m + 1]) for m in range(0, coarse_cols, 2)], axis=1
        )
        strips[k] = strip
        high, low = split(strip)
        right = jnp.concatenate([high, high, low, low], axis=0)
        wide = weights[k]
        terms = jnp.dot(jnp.concatenate([wide, wide], axis=1), right, preferred_element_type=f32)
        for source in range(n_sources):
            part[goals[source, k]] += terms[source * tile : (source + 1) * tile]
    keep[...] = part[: n_chips * owned]
    send[...] = part[n_chips * owned : 2 * n_chips * owned]


def write_product(strips, product):
    fine_rows, coarse_cols, tile = product.shape[:3]
    for k in range(fine_rows):
        for m in range(coarse_cols):
            product[k, m] = strips[k, :, m * tile : (m + 1) * tile]


def add_pair(keep, received, *outs):
    owned = outs[0].shape[0]
    for m, out in enumerate(outs):
        out[...] = keep[m * owned : (m + 1) * owned] + received[m * owned : (m + 1) * owned]


def add_all(*refs):
    *parts, out = refs
    total = parts[0][...]
    for part in parts[1:]:
        total = total + part[...]
    tile = out.shape[2]
    for j in range(out.shape[0]):
        for m in range(out.shape[1]):
            out[j, m] = total[j, :, m * tile : (m + 1) * tile]


def swap(x, axis, mask):
    n = lax.axis_size(axis)
    return lax.ppermute(x, axis, [(i, i ^ mask) for i in range(n)])


def line_hops(own, step, before):
    n = lax.axis_size("col")

    def hop(x, first):
        pairs = []
        for i in range(first, n - 1, 2):
            if i - (step - 1) >= 0:
                pairs.append((i, i + 1))
            if i + step <= n - 1:
                pairs.append((i + 1, i))
        return lax.ppermute(x, "col", pairs) if pairs else None

    found = {}
    for name, other, first in (("even", "odd", 0), ("odd", "even", 1)):
        x = own if step == 1 else before.get((other, step - 1))
        found[name, step] = hop(x, first) if x is not None else None
    return {key: x for key, x in found.items() if x is not None}


def shards(op_tiles, op_rows, op_cols, op_count, pro_tiles, pro_cols, pro_live):
    list_len, tile = op_tiles.shape[0], op_tiles.shape[2]
    fine_rows = pro_tiles.shape[0]
    row_count, col_count = lax.axis_size("row"), lax.axis_size("col")
    fine_total = fine_rows * row_count
    fine_cols = fine_total // col_count
    coarse_total = fine_total // COARSEN
    coarse_cols = coarse_total // col_count
    owned = coarse_total // row_count
    n_chips = row_count // 2
    sizes = (tile, list_len, fine_rows, coarse_cols, fine_total, owned)
    first_rows = (GROUP // 2 + fine_rows // 2) * tile + META
    z_rows = first_rows + (list_len - GROUP) // 2 * tile
    r_rows = fine_rows // 2 * tile + META

    z_pay, r_pay = call(
        functools.partial(pack, fine_cols, coarse_cols),
        (shape(z_rows, 2 * tile), shape(r_rows, 2 * tile)),
        7,
        (
            pltpu.VMEM(pro_tiles.shape, f32),
            pltpu.VMEM((1, list_len), i32),
            pltpu.VMEM((1, list_len), i32),
            pltpu.VMEM((1, 1), i32),
            pltpu.VMEM((1, fine_rows), i32),
            pltpu.VMEM((1, fine_rows), i32),
            pltpu.VMEM((GROUP,) + op_tiles.shape[1:], f32),
            pltpu.VMEM((list_len - GROUP,) + op_tiles.shape[1:], f32),
            pltpu.SemaphoreType.DMA((8,)),
        ),
        nbytes=4 * 2**20,
        space=HBM,
        limit=FULL_BYTES,
    )(
        op_tiles,
        pro_tiles,
        op_rows.reshape(1, -1),
        op_cols.reshape(1, -1),
        op_count,
        pro_cols.reshape(1, -1),
        pro_live.reshape(1, -1),
    )

    found = [line_hops(z_pay, 1, {})]
    for step in range(2, col_count):
        found.append(line_hops(z_pay, step, found[-1]))
    chips = [r_pay] + [swap(r_pay, "row", m) for m in range(2, row_count, 2)]
    panel_pays = [x for pair in zip(chips, [swap(x, "row", 1) for x in chips]) for x in pair]

    def stage(first, last, n_prev, state, pays):
        n_all = n_prev + len(pays)
        out = [
            shape(fine_rows * coarse_cols, tile, 2 * tile),
            shape(fine_rows, col_count * tile, 2 * tile, dtype=bf16),
            shape(n_all, META, 2 * tile),
        ]
        scratch = [
            pltpu.SMEM((row_count, META, 2 * tile), f32),
            pltpu.SMEM((n_all, META, 2 * tile), f32),
            pltpu.SemaphoreType.DMA((row_count + n_all + 2,)),
        ]
        if first:
            out += [shape(fine_total + 1, tile, 2 * tile, dtype=bf16), shape(row_count, META, 2 * tile)]
        if last:
            spread = n_chips * owned
            scratch = [
                pltpu.VMEM(out[0].shape, f32),
                pltpu.VMEM(out[1].shape, bf16),
                pltpu.VMEM((2 * spread + 1, tile, coarse_cols * tile), f32),
                pltpu.SMEM((col_count, fine_rows), i32),
            ] + scratch
            out = [shape(fine_rows, tile, coarse_cols * tile)] + [shape(spread, tile, coarse_cols * tile)] * 2
        operands = list(state) + list(pays)
        kernel = functools.partial(products, first, last, row_count, n_prev, len(pays), sizes)
        return call(kernel, tuple(out), len(operands), scratch, flops=2**28, nbytes=4 * 2**20)(*operands)

    early = [z_pay] + list(found[0].values())
    middle = [x for step in found[1:-1] for x in step.values()]
    late = list(found[-1].values())
    acc, weights, metas, panel, ids = stage(True, False, 0, panel_pays, early)
    acc, weights, metas = stage(False, False, len(early), (acc, panel, weights, ids, metas), middle)
    strips, keep, send = stage(False, True, len(early + middle), (acc, panel, weights, ids, metas), late)

    received = swap(send, "row", 1)
    product = call(
        write_product, shape(fine_rows, coarse_cols, tile, tile), 1, flops=2**24, nbytes=2**20
    )(strips)
    part = shape(owned, tile, coarse_cols * tile)
    parts = call(add_pair, (part,) * n_chips, 2, nbytes=2**20)(keep, received)
    others = [swap(parts[m], "row", 2 * m) for m in range(1, n_chips)]
    coarse = call(add_all, shape(owned, coarse_cols, tile, tile), n_chips, nbytes=2**20)(parts[0], *others)
    return (product, coarse)


def solution(mesh):
    return jax.shard_map(
        shards,
        mesh=mesh,
        in_specs=(
            P("row", "col", None, None),
            P("row", "col"),
            P("row", "col"),
            P("row", "col"),
            P("row", "col", None, None),
            P("row", "col"),
            P("row", "col"),
        ),
        out_specs=(P("row", "col", None, None), P("row", "col", None, None)),
        check_vma=False,
    )
```

```python
import functools

import jax
import jax.numpy as jnp
from jax import lax
from jax.experimental import pallas as pl
from jax.experimental.pallas import tpu as pltpu
from jax.sharding import PartitionSpec as P

COARSEN = 4
GROUP = 16
META = 8
VMEM_BYTES = 48 * 2**20
FULL_BYTES = 63 * 2**20

f32, bf16, i32 = jnp.float32, jnp.bfloat16, jnp.int32
VMEM = pl.BlockSpec(memory_space=pltpu.VMEM)
HBM = pl.BlockSpec(memory_space=pltpu.HBM)


def call(kernel, out_shape, n_in, scratch=(), flops=0, nbytes=0, space=VMEM, limit=VMEM_BYTES):
    return pl.pallas_call(
        kernel,
        out_shape=out_shape,
        in_specs=[space] * n_in,
        out_specs=jax.tree.map(lambda _: VMEM, out_shape),
        scratch_shapes=list(scratch),
        compiler_params=pltpu.CompilerParams(vmem_limit_bytes=limit),
        cost_estimate=pl.CostEstimate(flops=flops, bytes_accessed=nbytes, transcendentals=0),
    )


def shape(*dims, dtype=f32):
    return jax.ShapeDtypeStruct(dims, dtype)


def divide(x, n):
    if n & (n - 1):
        return x // n, x % n
    return lax.shift_right_logical(x, n.bit_length() - 1), x & (n - 1)


def pack(fine_cols, coarse_cols, op, pro, rows, cols, count, pro_cols, pro_live, whole, low, high, r_pay, *scratch):
    sems = scratch[-1]
    sources = (pro, rows, cols, count, pro_cols, pro_live, op.at[pl.ds(0, GROUP)], op.at[pl.ds(GROUP, op.shape[0] - GROUP)])
    copies = [pltpu.make_async_copy(src, dst, sems.at[i]) for i, (src, dst) in enumerate(zip(sources, scratch))]
    for copy in copies:
        copy.start()
    for copy in copies[:-2]:
        copy.wait()
    pro, rows, cols, count, pro_cols, pro_live, low_tiles, high_tiles = scratch[:-1]
    list_len, tile = op.shape[0], op.shape[2]
    fine_rows = pro.shape[0]
    half, quarter = GROUP // 2, fine_rows // 2
    col_index = lax.axis_index("col")
    base = half * tile
    eighth = quarter // 2
    meta = base + eighth * tile
    high_at = meta + META
    high_base = (list_len - GROUP) // 2 * tile
    for k in range(quarter):
        pair = jnp.concatenate([pro[k, 0], pro[k + quarter, 0]], axis=1)
        r_pay[k * tile : (k + 1) * tile, :] = pair
        turned = pair.T
        turned = jnp.concatenate([turned[:tile], turned[tile:]], axis=1)
        part, at = (low, base + k * tile) if k < eighth else (high, high_base + (k - eighth) * tile)
        part[at : at + tile, :] = turned
        at += 0 if k < eighth else high_at
        whole[at : at + tile, :] = turned
    r_pay[quarter * tile : quarter * tile + META, :] = jnp.zeros((META, 2 * tile), f32)
    live = pro_live[...] > 0
    r_pay[quarter * tile : quarter * tile + 1, 0:fine_rows] = jnp.where(live, pro_cols[...], -1).astype(f32)
    goals = jnp.where(live, pro_cols[...] + col_index * coarse_cols, -1).astype(f32)
    for pay in (whole, low):
        pay[meta : meta + META, :] = jnp.zeros((META, 2 * tile), f32)
        pay[meta : meta + 1, 0:list_len] = rows[...].astype(f32)
        pay[meta + 1 : meta + 2, 0:list_len] = (cols[...] + col_index * fine_cols).astype(f32)
        pay[meta + 2 : meta + 3, 0:1] = count[...].astype(f32)
        pay[meta + 2 : meta + 3, 1:2] = jnp.full((1, 1), col_index, i32).astype(f32)
        pay[meta + 3 : meta + 4, 0:fine_rows] = goals
    copies[-2].wait()
    for block in range(half):
        both = jnp.concatenate([low_tiles[block, 0], low_tiles[block + half, 0]], axis=1)
        for pay in (whole, low):
            pay[block * tile : (block + 1) * tile, :] = both
    copies[-1].wait()
    for block in range((list_len - GROUP) // 2):
        slot = block // half * GROUP + block % half
        both = jnp.concatenate([high_tiles[slot, 0], high_tiles[slot + half, 0]], axis=1)
        high[block * tile : (block + 1) * tile, :] = both
        whole[high_at + block * tile : high_at + (block + 1) * tile, :] = both


def split(x):
    high = x.astype(bf16)
    return high, (x - high.astype(f32)).astype(bf16)


def halves(pair):
    tile = pair.shape[0]
    high = pair.astype(bf16).astype(f32)
    low = pair - high
    left = lax.broadcasted_iota(i32, pair.shape, 1) < tile
    first = jnp.where(left, high, pltpu.roll(low, tile, 1))
    second = jnp.where(left, pltpu.roll(high, tile, 1), low)
    return first.astype(bf16), second.astype(bf16)


def add_products(low_pay, high_pay, high_at, meta, ids, panel, sizes, acc):
    tile, list_len, fine_rows, coarse_cols, fine_total, owned = sizes
    count = meta[2, 0].astype(i32)
    half = GROUP // 2
    row_index = lax.axis_index("row")
    for group in range(list_len // GROUP):
        blocks = high_pay if group else low_pay

        @pl.when(count > group * GROUP)
        def _(group=group):
            for p in range(half):
                at = p * tile + (high_at + (group - 1) * half * tile if group else 0)
                high, low = split(blocks[at : at + tile, :])
                left = jnp.concatenate([high, low], axis=0)
                rights, places = [], []
                for slot in (group * GROUP + p, group * GROUP + p + half):
                    fine = meta[1, slot].astype(i32)
                    shard, within = divide(fine, fine_rows)
                    target = ids[shard ^ row_index, 0, within].astype(i32)
                    live = jnp.logical_and(slot < count, target >= 0)
                    rights.append(panel[jnp.where(live, fine, fine_total)])
                    places.append(jnp.where(live, meta[0, slot].astype(i32) * coarse_cols + target, 0))
                empty = jnp.zeros_like(rights[0])
                right = jnp.concatenate(
                    [jnp.concatenate([rights[0], empty], axis=0), jnp.concatenate([empty, rights[1]], axis=0)], axis=1
                )
                prods = jnp.dot(left, right, preferred_element_type=f32)
                for side, place in enumerate(places):
                    part = prods[:, side * 2 * tile : (side + 1) * 2 * tile]
                    acc[place] += part[:tile] + part[tile:]


def products(first, last, n_panel, n_prev, parts, sizes, *refs):
    tile, list_len, fine_rows, coarse_cols, fine_total, owned = sizes
    refs = list(refs)
    take = lambda n: [refs.pop(0) for _ in range(n)]
    if first:
        r_pays = take(n_panel)
    else:
        acc_in, panel, weights_in, ids_in, metas_in = take(5)
    pays = [take(n) for n in parts]
    if last:
        strips, keep, send = take(3)
        acc, weights, part, goals = take(4)
    elif first:
        acc, weights, metas_out, panel, ids_out = take(5)
    else:
        acc, weights, metas_out = take(3)
    ids, metas, sems = take(3)
    half, quarter = GROUP // 2, fine_rows // 2
    n_all = n_prev + len(pays)
    row_index = lax.axis_index("row")
    eighth = quarter // 2
    meta_at = (half + eighth) * tile
    high_base = (list_len - GROUP) // 2 * tile

    moves = [(pay[0].at[pl.ds(meta_at, META)], metas.at[n_prev + i]) for i, pay in enumerate(pays)]
    if first:
        moves += [(pay.at[pl.ds(quarter * tile, META)], ids.at[m]) for m, pay in enumerate(r_pays)]
    else:
        moves += [(ids_in, ids), (metas_in, metas.at[pl.ds(0, n_prev)])]
    copies = [pltpu.make_async_copy(src, dst, sems.at[i]) for i, (src, dst) in enumerate(moves)]
    for copy in copies:
        copy.start()
    if first:
        acc[...] = jnp.zeros_like(acc)
        panel[fine_total] = jnp.zeros((tile, 2 * tile), bf16)
        for m, pay in enumerate(r_pays):
            at = (row_index ^ m) * fine_rows
            for k in range(quarter):
                panel[at + k], panel[at + k + quarter] = halves(pay[k * tile : (k + 1) * tile, :])
            ids_out[m] = pay[quarter * tile : quarter * tile + META, :]
    else:
        acc[...] = acc_in[...]
        weights[...] = weights_in[...]
    if not last:
        if n_prev:
            metas_out[:n_prev] = metas_in[...]
        for i, pay in enumerate(pays):
            metas_out[n_prev + i] = pay[0][meta_at : meta_at + META, :]
    for copy in copies:
        copy.wait()

    for i, pay in enumerate(pays):
        meta = metas.at[n_prev + i]

        @pl.when(meta[2, 0] > 0)
        def _(pay=pay, meta=meta):
            at = pl.multiple_of(meta[2, 1].astype(i32) * tile, tile)
            for k in range(quarter):
                if k < eighth:
                    block = pay[0][(half + k) * tile : (half + k + 1) * tile, :]
                else:
                    from_row = high_base + (k - eighth) * tile + (0 if len(pay) > 1 else meta_at + META)
                    block = pay[-1][from_row : from_row + tile, :]
                for kk, wide in zip((k, k + quarter), halves(block)):
                    weights[kk, pl.ds(at, tile), :] = wide

        high_at = 0 if len(pay) > 1 else meta_at + META
        add_products(pay[0], pay[-1], high_at, meta, ids, panel, sizes, acc)
    if not last:
        return

    dump = part.shape[0] - 1
    n_chips = keep.shape[0] // owned
    for i in range(n_all):

        @pl.when(metas[i, 2, 0] > 0)
        def _(i=i):
            source = metas[i, 2, 1].astype(i32)
            for k in range(fine_rows):
                goal = metas[i, 3, k].astype(i32)
                owner, within = divide(jnp.maximum(goal, 0), owned)
                chip, core = divide(owner ^ row_index, 2)
                goals[source, k] = jnp.where(goal >= 0, (core * n_chips + chip) * owned + within, dump)

    part[...] = jnp.zeros_like(part)
    n_sources = weights.shape[1] // tile
    for k in range(fine_rows):
        sums = []
        for m in range(coarse_cols):
            both = acc[k * coarse_cols + m]
            sums.append(both + pltpu.roll(both, tile, 1))
        left = lax.broadcasted_iota(i32, sums[0].shape, 1) < tile
        strip = jnp.concatenate(
            [jnp.where(left, sums[m], sums[m + 1]) for m in range(0, coarse_cols, 2)], axis=1
        )
        strips[k] = strip
        high, low = split(strip)
        right = jnp.concatenate([high, high, low, low], axis=0)
        wide = weights[k]
        terms = jnp.dot(jnp.concatenate([wide, wide], axis=1), right, preferred_element_type=f32)
        for source in range(n_sources):
            part[goals[source, k]] += terms[source * tile : (source + 1) * tile]
    keep[...] = part[: n_chips * owned]
    send[...] = part[n_chips * owned : 2 * n_chips * owned]


def write_product(strips, product):
    fine_rows, coarse_cols, tile = product.shape[:3]
    for k in range(fine_rows):
        for m in range(coarse_cols):
            product[k, m] = strips[k, :, m * tile : (m + 1) * tile]


def add_pair(keep, received, *outs):
    owned = outs[0].shape[0]
    for m, out in enumerate(outs):
        out[...] = keep[m * owned : (m + 1) * owned] + received[m * owned : (m + 1) * owned]


def add_all(*refs):
    *parts, out = refs
    total = parts[0][...]
    for part in parts[1:]:
        total = total + part[...]
    tile = out.shape[2]
    for j in range(out.shape[0]):
        for m in range(out.shape[1]):
            out[j, m] = total[j, :, m * tile : (m + 1) * tile]


def swap(x, axis, mask):
    n = lax.axis_size(axis)
    return lax.ppermute(x, axis, [(i, i ^ mask) for i in range(n)])


def line_gather(own, odd, hook=None):
    n = lax.axis_size("col")
    found = []
    for step in range(1, n):
        pairs = []
        for i in range((step - 1 + odd) % 2, n - 1, 2):
            if i - (step - 1) >= 0:
                pairs.append((i, i + 1))
            if i + step <= n - 1:
                pairs.append((i + 1, i))
        if not pairs:
            break
        own = lax.ppermute(own, "col", pairs)
        if step == 2 and hook is not None:
            own, *rest = lax.optimization_barrier((own, *hook))
            hook[:] = rest
        found.append(own)
    return found


def shards(op_tiles, op_rows, op_cols, op_count, pro_tiles, pro_cols, pro_live):
    list_len, tile = op_tiles.shape[0], op_tiles.shape[2]
    fine_rows = pro_tiles.shape[0]
    row_count, col_count = lax.axis_size("row"), lax.axis_size("col")
    fine_total = fine_rows * row_count
    fine_cols = fine_total // col_count
    coarse_total = fine_total // COARSEN
    coarse_cols = coarse_total // col_count
    owned = coarse_total // row_count
    n_chips = row_count // 2
    sizes = (tile, list_len, fine_rows, coarse_cols, fine_total, owned)
    first_rows = (GROUP // 2 + fine_rows // 4) * tile + META
    z_rows = (list_len // 2 + fine_rows // 2) * tile + META
    r_rows = fine_rows // 2 * tile + META

    whole, low, high, r_pay = call(
        functools.partial(pack, fine_cols, coarse_cols),
        (shape(z_rows, 2 * tile), shape(first_rows, 2 * tile), shape(z_rows - first_rows, 2 * tile), shape(r_rows, 2 * tile)),
        7,
        (
            pltpu.VMEM(pro_tiles.shape, f32),
            pltpu.VMEM((1, list_len), i32),
            pltpu.VMEM((1, list_len), i32),
            pltpu.VMEM((1, 1), i32),
            pltpu.VMEM((1, fine_rows), i32),
            pltpu.VMEM((1, fine_rows), i32),
            pltpu.VMEM((GROUP,) + op_tiles.shape[1:], f32),
            pltpu.VMEM((list_len - GROUP,) + op_tiles.shape[1:], f32),
            pltpu.SemaphoreType.DMA((8,)),
        ),
        nbytes=4 * 2**20,
        space=HBM,
        limit=FULL_BYTES,
    )(
        op_tiles,
        pro_tiles,
        op_rows.reshape(1, -1),
        op_cols.reshape(1, -1),
        op_count,
        pro_cols.reshape(1, -1),
        pro_live.reshape(1, -1),
    )

    chips = [r_pay] + [swap(r_pay, "row", m) for m in range(2, row_count, 2)]
    panel_pays = [x for pair in zip(chips, [swap(x, "row", 1) for x in chips]) for x in pair]

    split_chain = list(zip(line_gather(low, False, panel_pays), line_gather(high, False)))
    whole_chain = [(x,) for x in line_gather(whole, True)]
    def stage(first, last, n_prev, state, pays):
        n_all = n_prev + len(pays)
        out = [
            shape(fine_rows * coarse_cols, tile, 2 * tile),
            shape(fine_rows, col_count * tile, 2 * tile, dtype=bf16),
            shape(n_all, META, 2 * tile),
        ]
        scratch = [
            pltpu.SMEM((row_count, META, 2 * tile), f32),
            pltpu.SMEM((n_all, META, 2 * tile), f32),
            pltpu.SemaphoreType.DMA((row_count + n_all + 2,)),
        ]
        if first:
            out += [shape(fine_total + 1, tile, 2 * tile, dtype=bf16), shape(row_count, META, 2 * tile)]
        if last:
            spread = n_chips * owned
            scratch = [
                pltpu.VMEM(out[0].shape, f32),
                pltpu.VMEM(out[1].shape, bf16),
                pltpu.VMEM((2 * spread + 1, tile, coarse_cols * tile), f32),
                pltpu.SMEM((col_count, fine_rows), i32),
            ] + scratch
            out = [shape(fine_rows, tile, coarse_cols * tile)] + [shape(spread, tile, coarse_cols * tile)] * 2
        operands = list(state) + [x for pay in pays for x in pay]
        parts = [len(pay) for pay in pays]
        kernel = functools.partial(products, first, last, row_count, n_prev, parts, sizes)
        return call(kernel, tuple(out), len(operands), scratch, flops=2**28, nbytes=4 * 2**20)(*operands)

    early = [(low, high)] + split_chain[:1] + whole_chain[:1]
    middle = split_chain[1:-1] + whole_chain[1:]
    late = split_chain[-1:]
    acc, weights, metas, panel, ids = stage(True, False, 0, panel_pays, early)
    acc, weights, metas = stage(False, False, len(early), (acc, panel, weights, ids, metas), middle)
    strips, keep, send = stage(False, True, len(early + middle), (acc, panel, weights, ids, metas), late)

    received = swap(send, "row", 1)
    product = call(
        write_product, shape(fine_rows, coarse_cols, tile, tile), 1, flops=2**24, nbytes=2**20
    )(strips)
    part = shape(owned, tile, coarse_cols * tile)
    parts = call(add_pair, (part,) * n_chips, 2, nbytes=2**20)(keep, received)
    others = [swap(parts[m], "row", 2 * m) for m in range(1, n_chips)]
    coarse = call(add_all, shape(owned, coarse_cols, tile, tile), n_chips, nbytes=2**20)(parts[0], *others)
    return (product, coarse)


def solution(mesh):
    return jax.shard_map(
        shards,
        mesh=mesh,
        in_specs=(
            P("row", "col", None, None),
            P("row", "col"),
            P("row", "col"),
            P("row", "col"),
            P("row", "col", None, None),
            P("row", "col"),
            P("row", "col"),
        ),
        out_specs=(P("row", "col", None, None), P("row", "col", None, None)),
        check_vma=False,
    )
```

```python
import functools

import jax
import jax.numpy as jnp
from jax import lax
from jax.experimental import pallas as pl
from jax.experimental.pallas import tpu as pltpu
from jax.sharding import PartitionSpec as P

COARSEN = 4
GROUP = 16
META = 8
VMEM_BYTES = 48 * 2**20
FULL_BYTES = 63 * 2**20

f32, bf16, i32 = jnp.float32, jnp.bfloat16, jnp.int32
VMEM = pl.BlockSpec(memory_space=pltpu.VMEM)
HBM = pl.BlockSpec(memory_space=pltpu.HBM)


def call(kernel, out_shape, n_in, scratch=(), flops=0, nbytes=0, space=VMEM, limit=VMEM_BYTES):
    return pl.pallas_call(
        kernel,
        out_shape=out_shape,
        in_specs=[space] * n_in,
        out_specs=jax.tree.map(lambda _: VMEM, out_shape),
        scratch_shapes=list(scratch),
        compiler_params=pltpu.CompilerParams(vmem_limit_bytes=limit),
        cost_estimate=pl.CostEstimate(flops=flops, bytes_accessed=nbytes, transcendentals=0),
    )


def shape(*dims, dtype=f32):
    return jax.ShapeDtypeStruct(dims, dtype)


def divide(x, n):
    if n & (n - 1):
        return x // n, x % n
    return lax.shift_right_logical(x, n.bit_length() - 1), x & (n - 1)


def pack(fine_cols, coarse_cols, op, pro, rows, cols, count, pro_cols, pro_live, whole, low, high, r_pay, *scratch):
    sems = scratch[-1]
    sources = (pro, rows, cols, count, pro_cols, pro_live, op.at[pl.ds(0, GROUP)], op.at[pl.ds(GROUP, op.shape[0] - GROUP)])
    copies = [pltpu.make_async_copy(src, dst, sems.at[i]) for i, (src, dst) in enumerate(zip(sources, scratch))]
    for copy in copies:
        copy.start()
    for copy in copies[:-2]:
        copy.wait()
    pro, rows, cols, count, pro_cols, pro_live, low_tiles, high_tiles = scratch[:-1]
    list_len, tile = op.shape[0], op.shape[2]
    fine_rows = pro.shape[0]
    half, quarter = GROUP // 2, fine_rows // 2
    col_index = lax.axis_index("col")
    base = half * tile
    eighth = quarter // 2
    meta = base + eighth * tile
    high_at = meta + META
    high_base = (list_len - GROUP) // 2 * tile
    for k in range(quarter):
        pair = jnp.concatenate([pro[k, 0], pro[k + quarter, 0]], axis=1)
        r_pay[k * tile : (k + 1) * tile, :] = pair
        turned = pair.T
        turned = jnp.concatenate([turned[:tile], turned[tile:]], axis=1)
        part, at = (low, base + k * tile) if k < eighth else (high, high_base + (k - eighth) * tile)
        part[at : at + tile, :] = turned
        at += 0 if k < eighth else high_at
        whole[at : at + tile, :] = turned
    r_pay[quarter * tile : quarter * tile + META, :] = jnp.zeros((META, 2 * tile), f32)
    live = pro_live[...] > 0
    r_pay[quarter * tile : quarter * tile + 1, 0:fine_rows] = jnp.where(live, pro_cols[...], -1).astype(f32)
    goals = jnp.where(live, pro_cols[...] + col_index * coarse_cols, -1).astype(f32)
    for pay in (whole, low):
        pay[meta : meta + META, :] = jnp.zeros((META, 2 * tile), f32)
        pay[meta : meta + 1, 0:list_len] = rows[...].astype(f32)
        pay[meta + 1 : meta + 2, 0:list_len] = (cols[...] + col_index * fine_cols).astype(f32)
        pay[meta + 2 : meta + 3, 0:1] = count[...].astype(f32)
        pay[meta + 3 : meta + 4, 0:fine_rows] = goals
        pay[meta + 3 : meta + 4, fine_rows : fine_rows + 1] = jnp.ones((1, 1), f32)
        pay[meta + 3 : meta + 4, fine_rows + 1 : fine_rows + 2] = jnp.full((1, 1), col_index, i32).astype(f32)
    copies[-2].wait()
    for block in range(half):
        both = jnp.concatenate([low_tiles[block, 0], low_tiles[block + half, 0]], axis=1)
        for pay in (whole, low):
            pay[block * tile : (block + 1) * tile, :] = both
    copies[-1].wait()
    for block in range((list_len - GROUP) // 2):
        slot = block // half * GROUP + block % half
        both = jnp.concatenate([high_tiles[slot, 0], high_tiles[slot + half, 0]], axis=1)
        high[block * tile : (block + 1) * tile, :] = both
        whole[high_at + block * tile : high_at + (block + 1) * tile, :] = both


def split(x):
    high = x.astype(bf16)
    return high, (x - high.astype(f32)).astype(bf16)


def halves(pair):
    tile = pair.shape[0]
    high = pair.astype(bf16).astype(f32)
    low = pair - high
    left = lax.broadcasted_iota(i32, pair.shape, 1) < tile
    first = jnp.where(left, high, pltpu.roll(low, tile, 1))
    second = jnp.where(left, pltpu.roll(high, tile, 1), low)
    return first.astype(bf16), second.astype(bf16)


def add_products(low_pay, high_pay, high_at, meta, ids, panel, sizes, acc):
    tile, list_len, fine_rows, coarse_cols, fine_total, owned = sizes
    count = meta[2, 0].astype(i32)
    half = GROUP // 2
    row_index = lax.axis_index("row")
    for group in range(list_len // GROUP):
        blocks = high_pay if group else low_pay

        @pl.when(count > group * GROUP)
        def _(group=group):
            for p in range(half):
                at = p * tile + (high_at + (group - 1) * half * tile if group else 0)
                high, low = split(blocks[at : at + tile, :])
                left = jnp.concatenate([high, low], axis=0)
                rights, places = [], []
                for slot in (group * GROUP + p, group * GROUP + p + half):
                    fine = meta[1, slot].astype(i32)
                    shard, within = divide(fine, fine_rows)
                    target = ids[shard ^ row_index, within].astype(i32)
                    live = jnp.logical_and(slot < count, target >= 0)
                    rights.append(panel[jnp.where(live, fine, fine_total)])
                    places.append(jnp.where(live, meta[0, slot].astype(i32) * coarse_cols + target, 0))
                empty = jnp.zeros_like(rights[0])
                right = jnp.concatenate(
                    [jnp.concatenate([rights[0], empty], axis=0), jnp.concatenate([empty, rights[1]], axis=0)], axis=1
                )
                prods = jnp.dot(left, right, preferred_element_type=f32)
                for side, place in enumerate(places):
                    part = prods[:, side * 2 * tile : (side + 1) * 2 * tile]
                    acc[place] += part[:tile] + part[tile:]


def products(first, last, n_panel, n_prev, parts, sizes, *refs):
    tile, list_len, fine_rows, coarse_cols, fine_total, owned = sizes
    refs = list(refs)
    take = lambda n: [refs.pop(0) for _ in range(n)]
    if first:
        r_pays = take(n_panel)
    else:
        acc_in, panel, weights_in, ids_in, goals_in = take(5)
    pays = [take(n) for n in parts]
    if last:
        strips, keep, send = take(3)
        acc, weights, part, places = take(4)
    elif first:
        acc, weights, goals_out, panel, ids_in = take(5)
    else:
        acc, weights, goals_out = take(3)
    ids, metas, goals, sems = take(4)
    half, quarter = GROUP // 2, fine_rows // 2
    row_index = lax.axis_index("row")
    eighth = quarter // 2
    meta_at = (half + eighth) * tile
    high_base = (list_len - GROUP) // 2 * tile

    if first:
        for m, pay in enumerate(r_pays):
            ids_in[m : m + 1, :] = pay[quarter * tile : quarter * tile + 1, :]
    moves = [(ids_in, ids)]
    moves += [(pay[0].at[pl.ds(meta_at, META)], metas.at[i]) for i, pay in enumerate(pays)]
    if last:
        moves += [(goals_in, goals)]
    copies = [pltpu.make_async_copy(src, dst, sems.at[i]) for i, (src, dst) in enumerate(moves)]
    for copy in copies:
        copy.start()
    if first:
        acc[...] = jnp.zeros_like(acc)
        panel[fine_total] = jnp.zeros((tile, 2 * tile), bf16)
        for m, pay in enumerate(r_pays):
            at = (row_index ^ m) * fine_rows
            for k in range(quarter):
                panel[at + k], panel[at + k + quarter] = halves(pay[k * tile : (k + 1) * tile, :])
    else:
        acc[...] = acc_in[...]
        weights[...] = weights_in[...]
    if not last:
        if not first:
            goals_out[...] = goals_in[...]
        for i, pay in enumerate(pays):
            goals_out[n_prev + i : n_prev + i + 1, :] = pay[0][meta_at + 3 : meta_at + 4, :]
    for copy in copies:
        copy.wait()

    for i, pay in enumerate(pays):
        meta = metas.at[i]

        @pl.when(meta[3, fine_rows] > 0)
        def _(pay=pay, meta=meta):
            at = pl.multiple_of(meta[3, fine_rows + 1].astype(i32) * tile, tile)
            for k in range(quarter):
                if k < eighth:
                    block = pay[0][(half + k) * tile : (half + k + 1) * tile, :]
                else:
                    from_row = high_base + (k - eighth) * tile + (0 if len(pay) > 1 else meta_at + META)
                    block = pay[-1][from_row : from_row + tile, :]
                for kk, wide in zip((k, k + quarter), halves(block)):
                    weights[kk, pl.ds(at, tile), :] = wide

        high_at = 0 if len(pay) > 1 else meta_at + META
        add_products(pay[0], pay[-1], high_at, meta, ids, panel, sizes, acc)
    if not last:
        return

    dump = part.shape[0] - 1
    n_chips = keep.shape[0] // owned
    for read in [goals.at[i] for i in range(n_prev)] + [metas.at[i, 3] for i in range(len(pays))]:

        @pl.when(read[fine_rows] > 0)
        def _(read=read):
            source = read[fine_rows + 1].astype(i32)
            for k in range(fine_rows):
                goal = read[k].astype(i32)
                owner, within = divide(jnp.maximum(goal, 0), owned)
                chip, core = divide(owner ^ row_index, 2)
                places[source, k] = jnp.where(goal >= 0, (core * n_chips + chip) * owned + within, dump)

    part[...] = jnp.zeros_like(part)
    n_sources = weights.shape[1] // tile
    for k in range(fine_rows):
        sums = []
        for m in range(coarse_cols):
            both = acc[k * coarse_cols + m]
            sums.append(both + pltpu.roll(both, tile, 1))
        left = lax.broadcasted_iota(i32, sums[0].shape, 1) < tile
        strip = jnp.concatenate(
            [jnp.where(left, sums[m], sums[m + 1]) for m in range(0, coarse_cols, 2)], axis=1
        )
        strips[k] = strip
        high, low = split(strip)
        right = jnp.concatenate([high, high, low, low], axis=0)
        wide = weights[k]
        terms = jnp.dot(jnp.concatenate([wide, wide], axis=1), right, preferred_element_type=f32)
        for source in range(n_sources):
            part[places[source, k]] += terms[source * tile : (source + 1) * tile]
    keep[...] = part[: n_chips * owned]
    send[...] = part[n_chips * owned : 2 * n_chips * owned]


def write_product(strips, product):
    fine_rows, coarse_cols, tile = product.shape[:3]
    for k in range(fine_rows):
        for m in range(coarse_cols):
            product[k, m] = strips[k, :, m * tile : (m + 1) * tile]


def add_pair(keep, received, *outs):
    owned = outs[0].shape[0]
    for m, out in enumerate(outs):
        out[...] = keep[m * owned : (m + 1) * owned] + received[m * owned : (m + 1) * owned]


def add_all(*refs):
    *parts, out = refs
    total = parts[0][...]
    for part in parts[1:]:
        total = total + part[...]
    tile = out.shape[2]
    for j in range(out.shape[0]):
        for m in range(out.shape[1]):
            out[j, m] = total[j, :, m * tile : (m + 1) * tile]


def swap(x, axis, mask):
    n = lax.axis_size(axis)
    return lax.ppermute(x, axis, [(i, i ^ mask) for i in range(n)])


def line_gather(own, odd, hook=None):
    n = lax.axis_size("col")
    found = []
    for step in range(1, n):
        pairs = []
        for i in range((step - 1 + odd) % 2, n - 1, 2):
            if i - (step - 1) >= 0:
                pairs.append((i, i + 1))
            if i + step <= n - 1:
                pairs.append((i + 1, i))
        if not pairs:
            break
        own = lax.ppermute(own, "col", pairs)
        if step == 2 and hook is not None:
            own, *rest = lax.optimization_barrier((own, *hook))
            hook[:] = rest
        found.append(own)
    return found


def shards(op_tiles, op_rows, op_cols, op_count, pro_tiles, pro_cols, pro_live):
    list_len, tile = op_tiles.shape[0], op_tiles.shape[2]
    fine_rows = pro_tiles.shape[0]
    row_count, col_count = lax.axis_size("row"), lax.axis_size("col")
    fine_total = fine_rows * row_count
    fine_cols = fine_total // col_count
    coarse_total = fine_total // COARSEN
    coarse_cols = coarse_total // col_count
    owned = coarse_total // row_count
    n_chips = row_count // 2
    sizes = (tile, list_len, fine_rows, coarse_cols, fine_total, owned)
    first_rows = (GROUP // 2 + fine_rows // 4) * tile + META
    z_rows = (list_len // 2 + fine_rows // 2) * tile + META
    r_rows = fine_rows // 2 * tile + META

    whole, low, high, r_pay = call(
        functools.partial(pack, fine_cols, coarse_cols),
        (shape(z_rows, 2 * tile), shape(first_rows, 2 * tile), shape(z_rows - first_rows, 2 * tile), shape(r_rows, 2 * tile)),
        7,
        (
            pltpu.VMEM(pro_tiles.shape, f32),
            pltpu.VMEM((1, list_len), i32),
            pltpu.VMEM((1, list_len), i32),
            pltpu.VMEM((1, 1), i32),
            pltpu.VMEM((1, fine_rows), i32),
            pltpu.VMEM((1, fine_rows), i32),
            pltpu.VMEM((GROUP,) + op_tiles.shape[1:], f32),
            pltpu.VMEM((list_len - GROUP,) + op_tiles.shape[1:], f32),
            pltpu.SemaphoreType.DMA((8,)),
        ),
        nbytes=4 * 2**20,
        space=HBM,
        limit=FULL_BYTES,
    )(
        op_tiles,
        pro_tiles,
        op_rows.reshape(1, -1),
        op_cols.reshape(1, -1),
        op_count,
        pro_cols.reshape(1, -1),
        pro_live.reshape(1, -1),
    )

    chips = [r_pay] + [swap(r_pay, "row", m) for m in range(2, row_count, 2)]
    panel_pays = [x for pair in zip(chips, [swap(x, "row", 1) for x in chips]) for x in pair]

    split_chain = list(zip(line_gather(low, False, panel_pays), line_gather(high, False)))
    whole_chain = [(x,) for x in line_gather(whole, True)]
    n_ids, n_goals = (-(-n // META) * META for n in (row_count, 2 * col_count))

    def stage(first, last, n_prev, state, pays):
        out = [
            shape(fine_rows * coarse_cols, tile, 2 * tile),
            shape(fine_rows, col_count * tile, 2 * tile, dtype=bf16),
            shape(n_goals, 2 * tile),
        ]
        scratch = [
            pltpu.SMEM((n_ids, 2 * tile), f32),
            pltpu.SMEM((len(pays), META, 2 * tile), f32),
            pltpu.SMEM((n_goals, 2 * tile), f32),
            pltpu.SemaphoreType.DMA((len(pays) + 2,)),
        ]
        if first:
            out += [shape(fine_total + 1, tile, 2 * tile, dtype=bf16), shape(n_ids, 2 * tile)]
        if last:
            spread = n_chips * owned
            scratch = [
                pltpu.VMEM(out[0].shape, f32),
                pltpu.VMEM(out[1].shape, bf16),
                pltpu.VMEM((2 * spread + 1, tile, coarse_cols * tile), f32),
                pltpu.SMEM((col_count, fine_rows), i32),
            ] + scratch
            out = [shape(fine_rows, tile, coarse_cols * tile)] + [shape(spread, tile, coarse_cols * tile)] * 2
        operands = list(state) + [x for pay in pays for x in pay]
        parts = [len(pay) for pay in pays]
        kernel = functools.partial(products, first, last, row_count, n_prev, parts, sizes)
        return call(kernel, tuple(out), len(operands), scratch, flops=2**28, nbytes=4 * 2**20)(*operands)

    early = [(low, high)] + split_chain[:1] + whole_chain[:1]
    middle = split_chain[1:-1] + whole_chain[1:]
    late = split_chain[-1:]
    acc, weights, goals, panel, ids = stage(True, False, 0, panel_pays, early)
    acc, weights, goals = stage(False, False, len(early), (acc, panel, weights, ids, goals), middle)
    strips, keep, send = stage(False, True, len(early + middle), (acc, panel, weights, ids, goals), late)

    received = swap(send, "row", 1)
    product = call(
        write_product, shape(fine_rows, coarse_cols, tile, tile), 1, flops=2**24, nbytes=2**20
    )(strips)
    part = shape(owned, tile, coarse_cols * tile)
    parts = call(add_pair, (part,) * n_chips, 2, nbytes=2**20)(keep, received)
    others = [swap(parts[m], "row", 2 * m) for m in range(1, n_chips)]
    coarse = call(add_all, shape(owned, coarse_cols, tile, tile), n_chips, nbytes=2**20)(parts[0], *others)
    return (product, coarse)


def solution(mesh):
    return jax.shard_map(
        shards,
        mesh=mesh,
        in_specs=(
            P("row", "col", None, None),
            P("row", "col"),
            P("row", "col"),
            P("row", "col"),
            P("row", "col", None, None),
            P("row", "col"),
            P("row", "col"),
        ),
        out_specs=(P("row", "col", None, None), P("row", "col", None, None)),
        check_vma=False,
    )
```

```python
import functools

import jax
import jax.numpy as jnp
from jax import lax
from jax.experimental import pallas as pl
from jax.experimental.pallas import tpu as pltpu
from jax.sharding import PartitionSpec as P

COARSEN = 4
GROUP = 16
META = 8
VMEM_BYTES = 48 * 2**20
FULL_BYTES = 63 * 2**20

f32, bf16, i32 = jnp.float32, jnp.bfloat16, jnp.int32
VMEM = pl.BlockSpec(memory_space=pltpu.VMEM)
HBM = pl.BlockSpec(memory_space=pltpu.HBM)


def call(kernel, out_shape, n_in, scratch=(), flops=0, nbytes=0, space=VMEM, limit=VMEM_BYTES):
    return pl.pallas_call(
        kernel,
        out_shape=out_shape,
        in_specs=[space] * n_in,
        out_specs=jax.tree.map(lambda _: VMEM, out_shape),
        scratch_shapes=list(scratch),
        compiler_params=pltpu.CompilerParams(vmem_limit_bytes=limit),
        cost_estimate=pl.CostEstimate(flops=flops, bytes_accessed=nbytes, transcendentals=0),
    )


def shape(*dims, dtype=f32):
    return jax.ShapeDtypeStruct(dims, dtype)


def divide(x, n):
    if n & (n - 1):
        return x // n, x % n
    return lax.shift_right_logical(x, n.bit_length() - 1), x & (n - 1)


def pack(fine_cols, coarse_cols, op, pro, rows, cols, count, pro_cols, pro_live, low, high, r_pay, *scratch):
    sems = scratch[-1]
    sources = (pro, rows, cols, count, pro_cols, pro_live, op.at[pl.ds(0, GROUP)], op.at[pl.ds(GROUP, op.shape[0] - GROUP)])
    copies = [pltpu.make_async_copy(src, dst, sems.at[i]) for i, (src, dst) in enumerate(zip(sources, scratch))]
    for copy in copies:
        copy.start()
    for copy in copies[:-2]:
        copy.wait()
    pro, rows, cols, count, pro_cols, pro_live, low_tiles, high_tiles = scratch[:-1]
    list_len, tile = op.shape[0], op.shape[2]
    fine_rows = pro.shape[0]
    half, quarter = GROUP // 2, fine_rows // 2
    col_index = lax.axis_index("col")
    base = half * tile
    eighth = quarter // 2
    meta = base + eighth * tile
    high_base = (list_len - GROUP) // 2 * tile
    for k in range(quarter):
        pair = jnp.concatenate([pro[k, 0], pro[k + quarter, 0]], axis=1)
        r_pay[k * tile : (k + 1) * tile, :] = pair
        turned = pair.T
        turned = jnp.concatenate([turned[:tile], turned[tile:]], axis=1)
        part, at = (low, base + k * tile) if k < eighth else (high, high_base + (k - eighth) * tile)
        part[at : at + tile, :] = turned
    r_pay[quarter * tile : quarter * tile + META, :] = jnp.zeros((META, 2 * tile), f32)
    live = pro_live[...] > 0
    r_pay[quarter * tile : quarter * tile + 1, 0:fine_rows] = jnp.where(live, pro_cols[...], -1).astype(f32)
    goals = jnp.where(live, pro_cols[...] + col_index * coarse_cols, -1).astype(f32)
    low[meta : meta + META, :] = jnp.zeros((META, 2 * tile), f32)
    low[meta : meta + 1, 0:list_len] = rows[...].astype(f32)
    low[meta + 1 : meta + 2, 0:list_len] = (cols[...] + col_index * fine_cols).astype(f32)
    low[meta + 2 : meta + 3, 0:1] = count[...].astype(f32)
    low[meta + 3 : meta + 4, 0:fine_rows] = goals
    low[meta + 3 : meta + 4, fine_rows : fine_rows + 1] = jnp.ones((1, 1), f32)
    low[meta + 3 : meta + 4, fine_rows + 1 : fine_rows + 2] = jnp.full((1, 1), col_index, i32).astype(f32)
    copies[-2].wait()
    for block in range(half):
        low[block * tile : (block + 1) * tile, :] = jnp.concatenate([low_tiles[block, 0], low_tiles[block + half, 0]], axis=1)
    copies[-1].wait()
    for block in range((list_len - GROUP) // 2):
        slot = block // half * GROUP + block % half
        high[block * tile : (block + 1) * tile, :] = jnp.concatenate([high_tiles[slot, 0], high_tiles[slot + half, 0]], axis=1)


def split(x):
    high = x.astype(bf16)
    return high, (x - high.astype(f32)).astype(bf16)


def halves(pair):
    tile = pair.shape[0]
    high = pair.astype(bf16).astype(f32)
    low = pair - high
    left = lax.broadcasted_iota(i32, pair.shape, 1) < tile
    first = jnp.where(left, high, pltpu.roll(low, tile, 1))
    second = jnp.where(left, pltpu.roll(high, tile, 1), low)
    return first.astype(bf16), second.astype(bf16)


def add_products(low_pay, high_pay, meta, ids, panel, sizes, acc):
    tile, list_len, fine_rows, coarse_cols, fine_total, owned = sizes
    count = meta[2, 0].astype(i32)
    half = GROUP // 2
    row_index = lax.axis_index("row")
    for group in range(list_len // GROUP):
        blocks = high_pay if group else low_pay

        @pl.when(count > group * GROUP)
        def _(group=group):
            for p in range(half):
                at = (p + max(group - 1, 0) * half) * tile
                high, low = split(blocks[at : at + tile, :])
                left = jnp.concatenate([high, low], axis=0)
                rights, places = [], []
                for slot in (group * GROUP + p, group * GROUP + p + half):
                    fine = meta[1, slot].astype(i32)
                    shard, within = divide(fine, fine_rows)
                    target = ids[shard ^ row_index, within].astype(i32)
                    live = jnp.logical_and(slot < count, target >= 0)
                    rights.append(panel[jnp.where(live, fine, fine_total)])
                    places.append(jnp.where(live, meta[0, slot].astype(i32) * coarse_cols + target, 0))
                empty = jnp.zeros_like(rights[0])
                right = jnp.concatenate(
                    [jnp.concatenate([rights[0], empty], axis=0), jnp.concatenate([empty, rights[1]], axis=0)], axis=1
                )
                prods = jnp.dot(left, right, preferred_element_type=f32)
                for side, place in enumerate(places):
                    part = prods[:, side * 2 * tile : (side + 1) * 2 * tile]
                    acc[place] += part[:tile] + part[tile:]


def products(first, last, n_panel, n_prev, n_new, sizes, *refs):
    tile, list_len, fine_rows, coarse_cols, fine_total, owned = sizes
    refs = list(refs)
    take = lambda n: [refs.pop(0) for _ in range(n)]
    if first:
        r_pays = take(n_panel)
    else:
        acc_in, panel, weights_in, ids_in, goals_in = take(5)
    pays = [take(2) for _ in range(n_new)]
    if last:
        strips, keep, send = take(3)
        acc, weights, part, places = take(4)
    elif first:
        acc, weights, goals_out, panel, ids_in = take(5)
    else:
        acc, weights, goals_out = take(3)
    ids, metas, goals, sems = take(4)
    half, quarter = GROUP // 2, fine_rows // 2
    row_index = lax.axis_index("row")
    eighth = quarter // 2
    meta_at = (half + eighth) * tile
    high_base = (list_len - GROUP) // 2 * tile

    if first:
        for m, pay in enumerate(r_pays):
            ids_in[m : m + 1, :] = pay[quarter * tile : quarter * tile + 1, :]
    moves = [(ids_in, ids)]
    moves += [(pay[0].at[pl.ds(meta_at, META)], metas.at[i]) for i, pay in enumerate(pays)]
    if last:
        moves += [(goals_in, goals)]
    copies = [pltpu.make_async_copy(src, dst, sems.at[i]) for i, (src, dst) in enumerate(moves)]
    for copy in copies:
        copy.start()
    if first:
        acc[...] = jnp.zeros_like(acc)
        panel[fine_total] = jnp.zeros((tile, 2 * tile), bf16)
        for m, pay in enumerate(r_pays):
            at = (row_index ^ m) * fine_rows
            for k in range(quarter):
                panel[at + k], panel[at + k + quarter] = halves(pay[k * tile : (k + 1) * tile, :])
    else:
        acc[...] = acc_in[...]
        weights[...] = weights_in[...]
    if not last:
        if not first:
            goals_out[...] = goals_in[...]
        for i, pay in enumerate(pays):
            goals_out[n_prev + i : n_prev + i + 1, :] = pay[0][meta_at + 3 : meta_at + 4, :]
    for copy in copies:
        copy.wait()

    for i, pay in enumerate(pays):
        meta = metas.at[i]

        @pl.when(meta[3, fine_rows] > 0)
        def _(pay=pay, meta=meta):
            at = pl.multiple_of(meta[3, fine_rows + 1].astype(i32) * tile, tile)
            for k in range(quarter):
                if k < eighth:
                    block = pay[0][(half + k) * tile : (half + k + 1) * tile, :]
                else:
                    block = pay[1][high_base + (k - eighth) * tile : high_base + (k - eighth + 1) * tile, :]
                for kk, wide in zip((k, k + quarter), halves(block)):
                    weights[kk, pl.ds(at, tile), :] = wide

        add_products(pay[0], pay[1], meta, ids, panel, sizes, acc)
    if not last:
        return

    dump = part.shape[0] - 1
    n_chips = keep.shape[0] // owned
    for read in [goals.at[i] for i in range(n_prev)] + [metas.at[i, 3] for i in range(len(pays))]:

        @pl.when(read[fine_rows] > 0)
        def _(read=read):
            source = read[fine_rows + 1].astype(i32)
            for k in range(fine_rows):
                goal = read[k].astype(i32)
                owner, within = divide(jnp.maximum(goal, 0), owned)
                chip, core = divide(owner ^ row_index, 2)
                places[source, k] = jnp.where(goal >= 0, (core * n_chips + chip) * owned + within, dump)

    part[...] = jnp.zeros_like(part)
    n_sources = weights.shape[1] // tile
    for k in range(fine_rows):
        sums = []
        for m in range(coarse_cols):
            both = acc[k * coarse_cols + m]
            sums.append(both + pltpu.roll(both, tile, 1))
        left = lax.broadcasted_iota(i32, sums[0].shape, 1) < tile
        strip = jnp.concatenate(
            [jnp.where(left, sums[m], sums[m + 1]) for m in range(0, coarse_cols, 2)], axis=1
        )
        strips[k] = strip
        high, low = split(strip)
        right = jnp.concatenate([high, high, low, low], axis=0)
        wide = weights[k]
        terms = jnp.dot(jnp.concatenate([wide, wide], axis=1), right, preferred_element_type=f32)
        for source in range(n_sources):
            part[places[source, k]] += terms[source * tile : (source + 1) * tile]
    keep[...] = part[: n_chips * owned]
    send[...] = part[n_chips * owned : 2 * n_chips * owned]


def write_product(strips, product):
    fine_rows, coarse_cols, tile = product.shape[:3]
    for k in range(fine_rows):
        for m in range(coarse_cols):
            product[k, m] = strips[k, :, m * tile : (m + 1) * tile]


def add_pair(keep, received, *outs):
    owned = outs[0].shape[0]
    for m, out in enumerate(outs):
        out[...] = keep[m * owned : (m + 1) * owned] + received[m * owned : (m + 1) * owned]


def add_all(*refs):
    *parts, out = refs
    total = parts[0][...]
    for part in parts[1:]:
        total = total + part[...]
    tile = out.shape[2]
    for j in range(out.shape[0]):
        for m in range(out.shape[1]):
            out[j, m] = total[j, :, m * tile : (m + 1) * tile]


def swap(x, axis, mask):
    n = lax.axis_size(axis)
    return lax.ppermute(x, axis, [(i, i ^ mask) for i in range(n)])


def hop(x, odd, step):
    n = lax.axis_size("col")
    pairs = []
    for i in range((step - 1 + odd) % 2, n - 1, 2):
        if i - (step - 1) >= 0:
            pairs.append((i, i + 1))
        if i + step <= n - 1:
            pairs.append((i + 1, i))
    return lax.ppermute(x, "col", pairs) if pairs else None


def shards(op_tiles, op_rows, op_cols, op_count, pro_tiles, pro_cols, pro_live):
    list_len, tile = op_tiles.shape[0], op_tiles.shape[2]
    fine_rows = pro_tiles.shape[0]
    row_count, col_count = lax.axis_size("row"), lax.axis_size("col")
    fine_total = fine_rows * row_count
    fine_cols = fine_total // col_count
    coarse_total = fine_total // COARSEN
    coarse_cols = coarse_total // col_count
    owned = coarse_total // row_count
    n_chips = row_count // 2
    sizes = (tile, list_len, fine_rows, coarse_cols, fine_total, owned)
    low_rows = (GROUP // 2 + fine_rows // 4) * tile + META
    high_rows = ((list_len - GROUP) // 2 + fine_rows // 4) * tile
    r_rows = fine_rows // 2 * tile + META

    low, high, r_pay = call(
        functools.partial(pack, fine_cols, coarse_cols),
        (shape(low_rows, 2 * tile), shape(high_rows, 2 * tile), shape(r_rows, 2 * tile)),
        7,
        (
            pltpu.VMEM(pro_tiles.shape, f32),
            pltpu.VMEM((1, list_len), i32),
            pltpu.VMEM((1, list_len), i32),
            pltpu.VMEM((1, 1), i32),
            pltpu.VMEM((1, fine_rows), i32),
            pltpu.VMEM((1, fine_rows), i32),
            pltpu.VMEM((GROUP,) + op_tiles.shape[1:], f32),
            pltpu.VMEM((list_len - GROUP,) + op_tiles.shape[1:], f32),
            pltpu.SemaphoreType.DMA((8,)),
        ),
        nbytes=4 * 2**20,
        space=HBM,
        limit=FULL_BYTES,
    )(
        op_tiles,
        pro_tiles,
        op_rows.reshape(1, -1),
        op_cols.reshape(1, -1),
        op_count,
        pro_cols.reshape(1, -1),
        pro_live.reshape(1, -1),
    )

    even = [[hop(x, 0, 1)] for x in (low, high)]
    odd = [[hop(x, 1, 1)] for x in (low, high)]
    odd[0][0], _ = lax.optimization_barrier((odd[0][0], even[0][0]))
    for chains, side in ((even, 0), (odd, 1)):
        for chain in chains:
            for step in range(2, col_count):
                x = hop(chain[-1], side, step)
                if x is not None:
                    chain.append(x)
    split_chain, other_chain = list(zip(*even)), list(zip(*odd))
    n_ids, n_goals = (-(-n // META) * META for n in (row_count, 2 * col_count))
    one = swap(r_pay, "row", 2)
    r_later, *rest = lax.optimization_barrier((r_pay, other_chain[1][0]))
    other_chain[1] = (rest[0], other_chain[1][1])
    chips = [r_pay, one] + [swap(r_later, "row", m) for m in range(4, row_count, 2)]
    chips, *rest = lax.optimization_barrier((chips, other_chain[1][1]))
    other_chain[1] = (other_chain[1][0], rest[0])
    panel_pays = [x for pair in zip(chips, [swap(x, "row", 1) for x in chips]) for x in pair]

    def stage(first, last, n_prev, state, pays):
        out = [
            shape(fine_rows * coarse_cols, tile, 2 * tile),
            shape(fine_rows, col_count * tile, 2 * tile, dtype=bf16),
            shape(n_goals, 2 * tile),
        ]
        scratch = [
            pltpu.SMEM((n_ids, 2 * tile), f32),
            pltpu.SMEM((len(pays), META, 2 * tile), f32),
            pltpu.SMEM((n_goals, 2 * tile), f32),
            pltpu.SemaphoreType.DMA((len(pays) + 2,)),
        ]
        if first:
            out += [shape(fine_total + 1, tile, 2 * tile, dtype=bf16), shape(n_ids, 2 * tile)]
        if last:
            spread = n_chips * owned
            scratch = [
                pltpu.VMEM(out[0].shape, f32),
                pltpu.VMEM(out[1].shape, bf16),
                pltpu.VMEM((2 * spread + 1, tile, coarse_cols * tile), f32),
                pltpu.SMEM((col_count, fine_rows), i32),
            ] + scratch
            out = [shape(fine_rows, tile, coarse_cols * tile)] + [shape(spread, tile, coarse_cols * tile)] * 2
        operands = list(state) + [x for pay in pays for x in pay]
        kernel = functools.partial(products, first, last, row_count, n_prev, len(pays), sizes)
        return call(kernel, tuple(out), len(operands), scratch, flops=2**28, nbytes=4 * 2**20)(*operands)

    early = [(low, high)] + split_chain[:1] + other_chain[:1]
    middle = split_chain[1:-1] + other_chain[1:]
    late = split_chain[-1:]
    acc, weights, goals, panel, ids = stage(True, False, 0, panel_pays, early)
    acc, weights, goals = stage(False, False, len(early), (acc, panel, weights, ids, goals), middle)
    strips, keep, send = stage(False, True, len(early + middle), (acc, panel, weights, ids, goals), late)

    received = swap(send, "row", 1)
    product = call(
        write_product, shape(fine_rows, coarse_cols, tile, tile), 1, flops=2**24, nbytes=2**20
    )(strips)
    part = shape(owned, tile, coarse_cols * tile)
    parts = call(add_pair, (part,) * n_chips, 2, nbytes=2**20)(keep, received)
    others = [swap(parts[m], "row", 2 * m) for m in range(1, n_chips)]
    coarse = call(add_all, shape(owned, coarse_cols, tile, tile), n_chips, nbytes=2**20)(parts[0], *others)
    return (product, coarse)


def solution(mesh):
    return jax.shard_map(
        shards,
        mesh=mesh,
        in_specs=(
            P("row", "col", None, None),
            P("row", "col"),
            P("row", "col"),
            P("row", "col"),
            P("row", "col", None, None),
            P("row", "col"),
            P("row", "col"),
        ),
        out_specs=(P("row", "col", None, None), P("row", "col", None, None)),
        check_vma=False,
    )
```

```python
import functools

import jax
import jax.numpy as jnp
from jax import lax
from jax.experimental import pallas as pl
from jax.experimental.pallas import tpu as pltpu
from jax.sharding import PartitionSpec as P

COARSEN = 4
GROUP = 16
META = 8
VMEM_BYTES = 48 * 2**20
FULL_BYTES = 63 * 2**20

f32, bf16, i32 = jnp.float32, jnp.bfloat16, jnp.int32
VMEM = pl.BlockSpec(memory_space=pltpu.VMEM)
HBM = pl.BlockSpec(memory_space=pltpu.HBM)


def call(kernel, out_shape, n_in, scratch=(), flops=0, nbytes=0, space=VMEM, limit=VMEM_BYTES, out_space=VMEM):
    return pl.pallas_call(
        kernel,
        out_shape=out_shape,
        in_specs=[space] * n_in,
        out_specs=jax.tree.map(lambda _: out_space, out_shape),
        scratch_shapes=list(scratch),
        compiler_params=pltpu.CompilerParams(vmem_limit_bytes=limit),
        cost_estimate=pl.CostEstimate(flops=flops, bytes_accessed=nbytes, transcendentals=0),
    )


def shape(*dims, dtype=f32):
    return jax.ShapeDtypeStruct(dims, dtype)


def divide(x, n):
    if n & (n - 1):
        return x // n, x % n
    return lax.shift_right_logical(x, n.bit_length() - 1), x & (n - 1)


def pack(fine_cols, coarse_cols, op, pro, rows, cols, count, pro_cols, pro_live, low_out, high_out, r_out, *scratch):
    low, high, r_pay, sems = scratch[-4:]
    scratch = scratch[:-4]
    outward = [
        pltpu.make_async_copy(src, dst, sems.at[len(scratch) + i])
        for i, (src, dst) in enumerate(((r_pay, r_out), (low, low_out), (high, high_out)))
    ]
    sources = (pro, rows, cols, count, pro_cols, pro_live, op.at[pl.ds(0, GROUP)], op.at[pl.ds(GROUP, op.shape[0] - GROUP)])
    copies = [pltpu.make_async_copy(src, dst, sems.at[i]) for i, (src, dst) in enumerate(zip(sources, scratch))]
    for copy in copies:
        copy.start()
    for copy in copies[:-2]:
        copy.wait()
    pro, rows, cols, count, pro_cols, pro_live, low_tiles, high_tiles = scratch
    list_len, tile = op.shape[0], op.shape[2]
    fine_rows = pro.shape[0]
    half, quarter = GROUP // 2, fine_rows // 2
    col_index = lax.axis_index("col")
    base = half * tile
    eighth = quarter // 2
    meta = base + eighth * tile
    high_base = (list_len - GROUP) // 2 * tile
    for k in range(quarter):
        pair = jnp.concatenate([pro[k, 0], pro[k + quarter, 0]], axis=1)
        r_pay[k * tile : (k + 1) * tile, :] = pair
        turned = pair.T
        turned = jnp.concatenate([turned[:tile], turned[tile:]], axis=1)
        part, at = (low, base + k * tile) if k < eighth else (high, high_base + (k - eighth) * tile)
        part[at : at + tile, :] = turned
    r_pay[quarter * tile : quarter * tile + META, :] = jnp.zeros((META, 2 * tile), f32)
    live = pro_live[...] > 0
    r_pay[quarter * tile : quarter * tile + 1, 0:fine_rows] = jnp.where(live, pro_cols[...], -1).astype(f32)
    goals = jnp.where(live, pro_cols[...] + col_index * coarse_cols, -1).astype(f32)
    low[meta : meta + META, :] = jnp.zeros((META, 2 * tile), f32)
    low[meta : meta + 1, 0:list_len] = rows[...].astype(f32)
    low[meta + 1 : meta + 2, 0:list_len] = (cols[...] + col_index * fine_cols).astype(f32)
    low[meta + 2 : meta + 3, 0:1] = count[...].astype(f32)
    low[meta + 3 : meta + 4, 0:fine_rows] = goals
    low[meta + 3 : meta + 4, fine_rows : fine_rows + 1] = jnp.ones((1, 1), f32)
    low[meta + 3 : meta + 4, fine_rows + 1 : fine_rows + 2] = jnp.full((1, 1), col_index, i32).astype(f32)
    outward[0].start()
    copies[-2].wait()
    for block in range(half):
        low[block * tile : (block + 1) * tile, :] = jnp.concatenate([low_tiles[block, 0], low_tiles[block + half, 0]], axis=1)
    outward[1].start()
    copies[-1].wait()
    for block in range((list_len - GROUP) // 2):
        slot = block // half * GROUP + block % half
        high[block * tile : (block + 1) * tile, :] = jnp.concatenate([high_tiles[slot, 0], high_tiles[slot + half, 0]], axis=1)
    outward[2].start()
    for copy in outward:
        copy.wait()


def split(x):
    high = x.astype(bf16)
    return high, (x - high.astype(f32)).astype(bf16)


def halves(pair):
    tile = pair.shape[0]
    high = pair.astype(bf16).astype(f32)
    low = pair - high
    left = lax.broadcasted_iota(i32, pair.shape, 1) < tile
    first = jnp.where(left, high, pltpu.roll(low, tile, 1))
    second = jnp.where(left, pltpu.roll(high, tile, 1), low)
    return first.astype(bf16), second.astype(bf16)


def add_products(low_pay, high_pay, meta, ids, panel, sizes, acc):
    tile, list_len, fine_rows, coarse_cols, fine_total, owned = sizes
    count = meta[2, 0].astype(i32)
    half = GROUP // 2
    row_index = lax.axis_index("row")
    for group in range(list_len // GROUP):
        blocks = high_pay if group else low_pay

        @pl.when(count > group * GROUP)
        def _(group=group):
            for p in range(half):
                at = (p + max(group - 1, 0) * half) * tile
                high, low = split(blocks[at : at + tile, :])
                left = jnp.concatenate([high, low], axis=0)
                rights, places = [], []
                for slot in (group * GROUP + p, group * GROUP + p + half):
                    fine = meta[1, slot].astype(i32)
                    shard, within = divide(fine, fine_rows)
                    target = ids[shard ^ row_index, within].astype(i32)
                    live = jnp.logical_and(slot < count, target >= 0)
                    rights.append(panel[jnp.where(live, fine, fine_total)])
                    places.append(jnp.where(live, meta[0, slot].astype(i32) * coarse_cols + target, 0))
                empty = jnp.zeros_like(rights[0])
                right = jnp.concatenate(
                    [jnp.concatenate([rights[0], empty], axis=0), jnp.concatenate([empty, rights[1]], axis=0)], axis=1
                )
                prods = jnp.dot(left, right, preferred_element_type=f32)
                for side, place in enumerate(places):
                    part = prods[:, side * 2 * tile : (side + 1) * 2 * tile]
                    acc[place] += part[:tile] + part[tile:]


def products(first, last, n_panel, n_prev, n_new, sizes, *refs):
    tile, list_len, fine_rows, coarse_cols, fine_total, owned = sizes
    refs = list(refs)
    take = lambda n: [refs.pop(0) for _ in range(n)]
    if first:
        r_pays = take(n_panel)
    else:
        acc_in, panel, weights_in, ids_in, goals_in = take(5)
    pays = [take(2) for _ in range(n_new)]
    if last:
        strips, keep, send = take(3)
        acc, weights, part, places = take(4)
    elif first:
        acc, weights, goals_out, panel, ids_in = take(5)
    else:
        acc, weights, goals_out = take(3)
    ids, metas, goals, sems = take(4)
    half, quarter = GROUP // 2, fine_rows // 2
    row_index = lax.axis_index("row")
    eighth = quarter // 2
    meta_at = (half + eighth) * tile
    high_base = (list_len - GROUP) // 2 * tile

    if first:
        for m, pay in enumerate(r_pays):
            ids_in[m : m + 1, :] = pay[quarter * tile : quarter * tile + 1, :]
    moves = [(ids_in, ids)]
    moves += [(pay[0].at[pl.ds(meta_at, META)], metas.at[i]) for i, pay in enumerate(pays)]
    if last:
        moves += [(goals_in, goals)]
    copies = [pltpu.make_async_copy(src, dst, sems.at[i]) for i, (src, dst) in enumerate(moves)]
    for copy in copies:
        copy.start()
    if first:
        acc[...] = jnp.zeros_like(acc)
        panel[fine_total] = jnp.zeros((tile, 2 * tile), bf16)
        for m, pay in enumerate(r_pays):
            at = (row_index ^ m) * fine_rows
            for k in range(quarter):
                panel[at + k], panel[at + k + quarter] = halves(pay[k * tile : (k + 1) * tile, :])
    else:
        acc[...] = acc_in[...]
        weights[...] = weights_in[...]
    if not last:
        if not first:
            goals_out[...] = goals_in[...]
        for i, pay in enumerate(pays):
            goals_out[n_prev + i : n_prev + i + 1, :] = pay[0][meta_at + 3 : meta_at + 4, :]
    if last:
        part[...] = jnp.zeros_like(part)
    for copy in copies:
        copy.wait()

    for i, pay in enumerate(pays):
        meta = metas.at[i]

        @pl.when(meta[3, fine_rows] > 0)
        def _(pay=pay, meta=meta):
            at = pl.multiple_of(meta[3, fine_rows + 1].astype(i32) * tile, tile)
            for k in range(quarter):
                if k < eighth:
                    block = pay[0][(half + k) * tile : (half + k + 1) * tile, :]
                else:
                    block = pay[1][high_base + (k - eighth) * tile : high_base + (k - eighth + 1) * tile, :]
                for kk, wide in zip((k, k + quarter), halves(block)):
                    weights[kk, pl.ds(at, tile), :] = wide

        add_products(pay[0], pay[1], meta, ids, panel, sizes, acc)
    if not last:
        return

    dump = part.shape[0] - 1
    n_chips = keep.shape[0] // owned
    for read in [goals.at[i] for i in range(n_prev)] + [metas.at[i, 3] for i in range(len(pays))]:

        @pl.when(read[fine_rows] > 0)
        def _(read=read):
            source = read[fine_rows + 1].astype(i32)
            for k in range(fine_rows):
                goal = read[k].astype(i32)
                owner, within = divide(jnp.maximum(goal, 0), owned)
                chip, core = divide(owner ^ row_index, 2)
                places[source, k] = jnp.where(goal >= 0, (core * n_chips + chip) * owned + within, dump)

    n_sources = weights.shape[1] // tile
    for k in range(fine_rows):
        sums = []
        for m in range(coarse_cols):
            both = acc[k * coarse_cols + m]
            sums.append(both + pltpu.roll(both, tile, 1))
        left = lax.broadcasted_iota(i32, sums[0].shape, 1) < tile
        strip = jnp.concatenate(
            [jnp.where(left, sums[m], sums[m + 1]) for m in range(0, coarse_cols, 2)], axis=1
        )
        strips[k] = strip
        high, low = split(strip)
        right = jnp.concatenate([high, high, low, low], axis=0)
        wide = weights[k]
        terms = jnp.dot(jnp.concatenate([wide, wide], axis=1), right, preferred_element_type=f32)
        for source in range(n_sources):
            part[places[source, k]] += terms[source * tile : (source + 1) * tile]
    keep[...] = part[: n_chips * owned]
    send[...] = part[n_chips * owned : 2 * n_chips * owned]


def write_product(strips, product):
    fine_rows, coarse_cols, tile = product.shape[:3]
    for k in range(fine_rows):
        for m in range(coarse_cols):
            product[k, m] = strips[k, :, m * tile : (m + 1) * tile]


def add_pair(keep, received, *outs):
    owned = outs[0].shape[0]
    for m, out in enumerate(outs):
        out[...] = keep[m * owned : (m + 1) * owned] + received[m * owned : (m + 1) * owned]


def add_all(*refs):
    *parts, out = refs
    total = parts[0][...]
    for part in parts[1:]:
        total = total + part[...]
    tile = out.shape[2]
    for j in range(out.shape[0]):
        for m in range(out.shape[1]):
            out[j, m] = total[j, :, m * tile : (m + 1) * tile]


def swap(x, axis, mask):
    n = lax.axis_size(axis)
    return lax.ppermute(x, axis, [(i, i ^ mask) for i in range(n)])


def hop(x, odd, step):
    n = lax.axis_size("col")
    pairs = []
    for i in range((step - 1 + odd) % 2, n - 1, 2):
        if i - (step - 1) >= 0:
            pairs.append((i, i + 1))
        if i + step <= n - 1:
            pairs.append((i + 1, i))
    return lax.ppermute(x, "col", pairs) if pairs else None


def shards(op_tiles, op_rows, op_cols, op_count, pro_tiles, pro_cols, pro_live):
    list_len, tile = op_tiles.shape[0], op_tiles.shape[2]
    fine_rows = pro_tiles.shape[0]
    row_count, col_count = lax.axis_size("row"), lax.axis_size("col")
    fine_total = fine_rows * row_count
    fine_cols = fine_total // col_count
    coarse_total = fine_total // COARSEN
    coarse_cols = coarse_total // col_count
    owned = coarse_total // row_count
    n_chips = row_count // 2
    sizes = (tile, list_len, fine_rows, coarse_cols, fine_total, owned)
    low_rows = (GROUP // 2 + fine_rows // 4) * tile + META
    high_rows = ((list_len - GROUP) // 2 + fine_rows // 4) * tile
    r_rows = fine_rows // 2 * tile + META

    low, high, r_pay = call(
        functools.partial(pack, fine_cols, coarse_cols),
        (shape(low_rows, 2 * tile), shape(high_rows, 2 * tile), shape(r_rows, 2 * tile)),
        7,
        (
            pltpu.VMEM(pro_tiles.shape, f32),
            pltpu.VMEM((1, list_len), i32),
            pltpu.VMEM((1, list_len), i32),
            pltpu.VMEM((1, 1), i32),
            pltpu.VMEM((1, fine_rows), i32),
            pltpu.VMEM((1, fine_rows), i32),
            pltpu.VMEM((GROUP,) + op_tiles.shape[1:], f32),
            pltpu.VMEM((list_len - GROUP,) + op_tiles.shape[1:], f32),
            pltpu.VMEM((low_rows, 2 * tile), f32),
            pltpu.VMEM((high_rows, 2 * tile), f32),
            pltpu.VMEM((r_rows, 2 * tile), f32),
            pltpu.SemaphoreType.DMA((11,)),
        ),
        nbytes=4 * 2**20,
        space=HBM,
        out_space=HBM,
        limit=FULL_BYTES,
    )(
        op_tiles,
        pro_tiles,
        op_rows.reshape(1, -1),
        op_cols.reshape(1, -1),
        op_count,
        pro_cols.reshape(1, -1),
        pro_live.reshape(1, -1),
    )

    even = [[hop(x, 0, 1)] for x in (low, high)]
    odd = [[hop(x, 1, 1)] for x in (low, high)]
    odd[0][0], _ = lax.optimization_barrier((odd[0][0], even[0][0]))
    for chains, side in ((even, 0), (odd, 1)):
        for chain in chains:
            for step in range(2, col_count):
                x = hop(chain[-1], side, step)
                if x is not None:
                    chain.append(x)
    split_chain, other_chain = list(zip(*even)), list(zip(*odd))
    n_ids, n_goals = (-(-n // META) * META for n in (row_count, 2 * col_count))
    one = swap(r_pay, "row", 2)
    r_later, *rest = lax.optimization_barrier((r_pay, other_chain[1][0]))
    other_chain[1] = (rest[0], other_chain[1][1])
    chips = [r_pay, one] + [swap(r_later, "row", m) for m in range(4, row_count, 2)]
    chips, *rest = lax.optimization_barrier((chips, other_chain[1][1]))
    other_chain[1] = (other_chain[1][0], rest[0])
    panel_pays = [x for pair in zip(chips, [swap(x, "row", 1) for x in chips]) for x in pair]

    def stage(first, last, n_prev, state, pays):
        out = [
            shape(fine_rows * coarse_cols, tile, 2 * tile),
            shape(fine_rows, col_count * tile, 2 * tile, dtype=bf16),
            shape(n_goals, 2 * tile),
        ]
        scratch = [
            pltpu.SMEM((n_ids, 2 * tile), f32),
            pltpu.SMEM((len(pays), META, 2 * tile), f32),
            pltpu.SMEM((n_goals, 2 * tile), f32),
            pltpu.SemaphoreType.DMA((len(pays) + 2,)),
        ]
        if first:
            out += [shape(fine_total + 1, tile, 2 * tile, dtype=bf16), shape(n_ids, 2 * tile)]
        if last:
            spread = n_chips * owned
            scratch = [
                pltpu.VMEM(out[0].shape, f32),
                pltpu.VMEM(out[1].shape, bf16),
                pltpu.VMEM((2 * spread + 1, tile, coarse_cols * tile), f32),
                pltpu.SMEM((col_count, fine_rows), i32),
            ] + scratch
            out = [shape(fine_rows, tile, coarse_cols * tile)] + [shape(spread, tile, coarse_cols * tile)] * 2
        operands = list(state) + [x for pay in pays for x in pay]
        kernel = functools.partial(products, first, last, row_count, n_prev, len(pays), sizes)
        return call(kernel, tuple(out), len(operands), scratch, flops=2**28, nbytes=4 * 2**20)(*operands)

    early = [(low, high)] + split_chain[:1] + other_chain[:1]
    middle = split_chain[1:-1] + other_chain[1:]
    late = split_chain[-1:]
    acc, weights, goals, panel, ids = stage(True, False, 0, panel_pays, early)
    acc, weights, goals = stage(False, False, len(early), (acc, panel, weights, ids, goals), middle)
    strips, keep, send = stage(False, True, len(early + middle), (acc, panel, weights, ids, goals), late)

    received = swap(send, "row", 1)
    product = call(
        write_product, shape(fine_rows, coarse_cols, tile, tile), 1, flops=2**24, nbytes=2**20
    )(strips)
    part = shape(owned, tile, coarse_cols * tile)
    parts = call(add_pair, (part,) * n_chips, 2, nbytes=2**20)(keep, received)
    others = [swap(parts[m], "row", 2 * m) for m in reversed(range(1, n_chips))]
    coarse = call(add_all, shape(owned, coarse_cols, tile, tile), n_chips, nbytes=2**20)(parts[0], *others)
    return (product, coarse)


def solution(mesh):
    return jax.shard_map(
        shards,
        mesh=mesh,
        in_specs=(
            P("row", "col", None, None),
            P("row", "col"),
            P("row", "col"),
            P("row", "col"),
            P("row", "col", None, None),
            P("row", "col"),
            P("row", "col"),
        ),
        out_specs=(P("row", "col", None, None), P("row", "col", None, None)),
        check_vma=False,
    )
```

```python
import functools

import jax
import jax.numpy as jnp
from jax import lax
from jax.experimental import pallas as pl
from jax.experimental.pallas import tpu as pltpu
from jax.sharding import PartitionSpec as P

COARSEN = 4
GROUP = 16
META = 8
VMEM_BYTES = 48 * 2**20
FULL_BYTES = 63 * 2**20

f32, bf16, i32 = jnp.float32, jnp.bfloat16, jnp.int32
VMEM = pl.BlockSpec(memory_space=pltpu.VMEM)
HBM = pl.BlockSpec(memory_space=pltpu.HBM)


def call(kernel, out_shape, n_in, scratch=(), flops=0, nbytes=0, space=VMEM, limit=VMEM_BYTES):
    return pl.pallas_call(
        kernel,
        out_shape=out_shape,
        in_specs=[space] * n_in,
        out_specs=jax.tree.map(lambda _: VMEM, out_shape),
        scratch_shapes=list(scratch),
        compiler_params=pltpu.CompilerParams(vmem_limit_bytes=limit),
        cost_estimate=pl.CostEstimate(flops=flops, bytes_accessed=nbytes, transcendentals=0),
    )


def shape(*dims, dtype=f32):
    return jax.ShapeDtypeStruct(dims, dtype)


def divide(x, n):
    if n & (n - 1):
        return x // n, x % n
    return lax.shift_right_logical(x, n.bit_length() - 1), x & (n - 1)


def pack(fine_cols, coarse_cols, op, pro, rows, cols, count, pro_cols, pro_live, low, high, r_pay, *scratch):
    sems = scratch[-1]
    sources = (pro, rows, cols, count, pro_cols, pro_live, op.at[pl.ds(0, GROUP)], op.at[pl.ds(GROUP, op.shape[0] - GROUP)])
    copies = [pltpu.make_async_copy(src, dst, sems.at[i]) for i, (src, dst) in enumerate(zip(sources, scratch))]
    for copy in copies:
        copy.start()
    for copy in copies[:-2]:
        copy.wait()
    pro, rows, cols, count, pro_cols, pro_live, low_tiles, high_tiles = scratch[:-1]
    list_len, tile = op.shape[0], op.shape[2]
    fine_rows = pro.shape[0]
    half, quarter = GROUP // 2, fine_rows // 2
    col_index = lax.axis_index("col")
    base = half * tile
    eighth = quarter // 2
    meta = base + eighth * tile
    high_base = (list_len - GROUP) // 2 * tile
    for k in range(quarter):
        pair = jnp.concatenate([pro[k, 0], pro[k + quarter, 0]], axis=1)
        r_pay[k * tile : (k + 1) * tile, :] = pair
        turned = pair.T
        turned = jnp.concatenate([turned[:tile], turned[tile:]], axis=1)
        part, at = (low, base + k * tile) if k < eighth else (high, high_base + (k - eighth) * tile)
        part[at : at + tile, :] = turned
    r_pay[quarter * tile : quarter * tile + META, :] = jnp.zeros((META, 2 * tile), f32)
    live = pro_live[...] > 0
    r_pay[quarter * tile : quarter * tile + 1, 0:fine_rows] = jnp.where(live, pro_cols[...], -1).astype(f32)
    goals = jnp.where(live, pro_cols[...] + col_index * coarse_cols, -1).astype(f32)
    low[meta : meta + META, :] = jnp.zeros((META, 2 * tile), f32)
    low[meta : meta + 1, 0:list_len] = rows[...].astype(f32)
    low[meta + 1 : meta + 2, 0:list_len] = (cols[...] + col_index * fine_cols).astype(f32)
    low[meta + 2 : meta + 3, 0:1] = count[...].astype(f32)
    low[meta + 3 : meta + 4, 0:fine_rows] = goals
    low[meta + 3 : meta + 4, fine_rows : fine_rows + 1] = jnp.ones((1, 1), f32)
    low[meta + 3 : meta + 4, fine_rows + 1 : fine_rows + 2] = jnp.full((1, 1), col_index, i32).astype(f32)
    copies[-2].wait()
    for block in range(half):
        low[block * tile : (block + 1) * tile, :] = jnp.concatenate([low_tiles[block, 0], low_tiles[block + half, 0]], axis=1)
    copies[-1].wait()
    for block in range((list_len - GROUP) // 2):
        slot = block // half * GROUP + block % half
        high[block * tile : (block + 1) * tile, :] = jnp.concatenate([high_tiles[slot, 0], high_tiles[slot + half, 0]], axis=1)


def split(x):
    high = x.astype(bf16)
    return high, (x - high.astype(f32)).astype(bf16)


def halves(pair):
    tile = pair.shape[0]
    high = pair.astype(bf16).astype(f32)
    low = pair - high
    left = lax.broadcasted_iota(i32, pair.shape, 1) < tile
    first = jnp.where(left, high, pltpu.roll(low, tile, 1))
    second = jnp.where(left, pltpu.roll(high, tile, 1), low)
    return first.astype(bf16), second.astype(bf16)


def add_products(low_pay, high_pay, meta, ids, panel, sizes, acc):
    tile, list_len, fine_rows, coarse_cols, fine_total, owned = sizes
    count = meta[2, 0].astype(i32)
    half = GROUP // 2
    row_index = lax.axis_index("row")
    for group in range(list_len // GROUP):
        blocks = high_pay if group else low_pay

        @pl.when(count > group * GROUP)
        def _(group=group):
            for p in range(half):
                at = (p + max(group - 1, 0) * half) * tile
                high, low = split(blocks[at : at + tile, :])
                left = jnp.concatenate([high, low], axis=0)
                rights, places = [], []
                for slot in (group * GROUP + p, group * GROUP + p + half):
                    fine = meta[1, slot].astype(i32)
                    shard, within = divide(fine, fine_rows)
                    target = ids[shard ^ row_index, within].astype(i32)
                    live = jnp.logical_and(slot < count, target >= 0)
                    rights.append(panel[jnp.where(live, fine, fine_total)])
                    places.append(jnp.where(live, meta[0, slot].astype(i32) * coarse_cols + target, 0))
                empty = jnp.zeros_like(rights[0])
                right = jnp.concatenate(
                    [jnp.concatenate([rights[0], empty], axis=0), jnp.concatenate([empty, rights[1]], axis=0)], axis=1
                )
                prods = jnp.dot(left, right, preferred_element_type=f32)
                for side, place in enumerate(places):
                    part = prods[:, side * 2 * tile : (side + 1) * 2 * tile]
                    acc[place] += part[:tile] + part[tile:]


def products(first, last, n_panel, n_prev, n_new, sizes, *refs):
    tile, list_len, fine_rows, coarse_cols, fine_total, owned = sizes
    refs = list(refs)
    take = lambda n: [refs.pop(0) for _ in range(n)]
    if first:
        r_pays = take(n_panel)
    else:
        acc_in, panel, weights_in, ids_in, goals_in = take(5)
    pays = [take(2) for _ in range(n_new)]
    if last:
        strips, keep, send = take(3)
        acc, weights, part, places = take(4)
    elif first:
        acc, weights, goals_out, panel, ids_in = take(5)
    else:
        acc, weights, goals_out = take(3)
    ids, metas, goals, sems = take(4)
    half, quarter = GROUP // 2, fine_rows // 2
    row_index = lax.axis_index("row")
    eighth = quarter // 2
    meta_at = (half + eighth) * tile
    high_base = (list_len - GROUP) // 2 * tile

    if first:
        for m, pay in enumerate(r_pays):
            ids_in[m : m + 1, :] = pay[quarter * tile : quarter * tile + 1, :]
    moves = [(ids_in, ids)]
    moves += [(pay[0].at[pl.ds(meta_at, META)], metas.at[i]) for i, pay in enumerate(pays)]
    if last:
        moves += [(goals_in, goals)]
    copies = [pltpu.make_async_copy(src, dst, sems.at[i]) for i, (src, dst) in enumerate(moves)]
    for copy in copies:
        copy.start()
    if first:
        acc[...] = jnp.zeros_like(acc)
        panel[fine_total] = jnp.zeros((tile, 2 * tile), bf16)
        for m, pay in enumerate(r_pays):
            at = (row_index ^ m) * fine_rows
            for k in range(quarter):
                panel[at + k], panel[at + k + quarter] = halves(pay[k * tile : (k + 1) * tile, :])
    else:
        acc[...] = acc_in[...]
        weights[...] = weights_in[...]
    if not last:
        if not first:
            goals_out[...] = goals_in[...]
        for i, pay in enumerate(pays):
            goals_out[n_prev + i : n_prev + i + 1, :] = pay[0][meta_at + 3 : meta_at + 4, :]
    for copy in copies:
        copy.wait()

    for i, pay in enumerate(pays):
        meta = metas.at[i]

        @pl.when(meta[3, fine_rows] > 0)
        def _(pay=pay, meta=meta):
            at = pl.multiple_of(meta[3, fine_rows + 1].astype(i32) * tile, tile)
            for k in range(quarter):
                if k < eighth:
                    block = pay[0][(half + k) * tile : (half + k + 1) * tile, :]
                else:
                    block = pay[1][high_base + (k - eighth) * tile : high_base + (k - eighth + 1) * tile, :]
                for kk, wide in zip((k, k + quarter), halves(block)):
                    weights[kk, pl.ds(at, tile), :] = wide

        add_products(pay[0], pay[1], meta, ids, panel, sizes, acc)
    if not last:
        return

    dump = part.shape[0] - 1
    n_chips = keep.shape[0] // owned
    for read in [goals.at[i] for i in range(n_prev)] + [metas.at[i, 3] for i in range(len(pays))]:

        @pl.when(read[fine_rows] > 0)
        def _(read=read):
            source = read[fine_rows + 1].astype(i32)
            for k in range(fine_rows):
                goal = read[k].astype(i32)
                owner, within = divide(jnp.maximum(goal, 0), owned)
                chip, core = divide(owner ^ row_index, 2)
                places[source, k] = jnp.where(goal >= 0, (core * n_chips + chip) * owned + within, dump)

    part[...] = jnp.zeros_like(part)
    n_sources = weights.shape[1] // tile
    for k in range(fine_rows):
        sums = []
        for m in range(coarse_cols):
            both = acc[k * coarse_cols + m]
            sums.append(both + pltpu.roll(both, tile, 1))
        left = lax.broadcasted_iota(i32, sums[0].shape, 1) < tile
        strip = jnp.concatenate(
            [jnp.where(left, sums[m], sums[m + 1]) for m in range(0, coarse_cols, 2)], axis=1
        )
        strips[k] = strip
        high, low = split(strip)
        right = jnp.concatenate([high, high, low, low], axis=0)
        wide = weights[k]
        terms = jnp.dot(jnp.concatenate([wide, wide], axis=1), right, preferred_element_type=f32)
        for source in range(n_sources):
            part[places[source, k]] += terms[source * tile : (source + 1) * tile]
    keep[...] = part[: n_chips * owned]
    send[...] = part[n_chips * owned : 2 * n_chips * owned]


def write_product(strips, product):
    fine_rows, coarse_cols, tile = product.shape[:3]
    for k in range(fine_rows):
        for m in range(coarse_cols):
            product[k, m] = strips[k, :, m * tile : (m + 1) * tile]


def add_pair(keep, received, *outs):
    owned = outs[0].shape[0]
    for m, out in enumerate(outs):
        out[...] = keep[m * owned : (m + 1) * owned] + received[m * owned : (m + 1) * owned]


def add_all(*refs):
    *parts, out = refs
    total = parts[0][...]
    for part in parts[1:]:
        total = total + part[...]
    tile = out.shape[2]
    for j in range(out.shape[0]):
        for m in range(out.shape[1]):
            out[j, m] = total[j, :, m * tile : (m + 1) * tile]


def swap(x, axis, mask):
    n = lax.axis_size(axis)
    return lax.ppermute(x, axis, [(i, i ^ mask) for i in range(n)])


def hop(x, odd, step):
    n = lax.axis_size("col")
    pairs = []
    for i in range((step - 1 + odd) % 2, n - 1, 2):
        if i - (step - 1) >= 0:
            pairs.append((i, i + 1))
        if i + step <= n - 1:
            pairs.append((i + 1, i))
    return lax.ppermute(x, "col", pairs) if pairs else None


def shards(op_tiles, op_rows, op_cols, op_count, pro_tiles, pro_cols, pro_live):
    list_len, tile = op_tiles.shape[0], op_tiles.shape[2]
    fine_rows = pro_tiles.shape[0]
    row_count, col_count = lax.axis_size("row"), lax.axis_size("col")
    fine_total = fine_rows * row_count
    fine_cols = fine_total // col_count
    coarse_total = fine_total // COARSEN
    coarse_cols = coarse_total // col_count
    owned = coarse_total // row_count
    n_chips = row_count // 2
    sizes = (tile, list_len, fine_rows, coarse_cols, fine_total, owned)
    low_rows = (GROUP // 2 + fine_rows // 4) * tile + META
    high_rows = ((list_len - GROUP) // 2 + fine_rows // 4) * tile
    r_rows = fine_rows // 2 * tile + META

    low, high, r_pay = call(
        functools.partial(pack, fine_cols, coarse_cols),
        (shape(low_rows, 2 * tile), shape(high_rows, 2 * tile), shape(r_rows, 2 * tile)),
        7,
        (
            pltpu.VMEM(pro_tiles.shape, f32),
            pltpu.VMEM((1, list_len), i32),
            pltpu.VMEM((1, list_len), i32),
            pltpu.VMEM((1, 1), i32),
            pltpu.VMEM((1, fine_rows), i32),
            pltpu.VMEM((1, fine_rows), i32),
            pltpu.VMEM((GROUP,) + op_tiles.shape[1:], f32),
            pltpu.VMEM((list_len - GROUP,) + op_tiles.shape[1:], f32),
            pltpu.SemaphoreType.DMA((8,)),
        ),
        nbytes=4 * 2**20,
        space=HBM,
        limit=FULL_BYTES,
    )(
        op_tiles,
        pro_tiles,
        op_rows.reshape(1, -1),
        op_cols.reshape(1, -1),
        op_count,
        pro_cols.reshape(1, -1),
        pro_live.reshape(1, -1),
    )

    even = [[hop(x, 0, 1)] for x in (low, high)]
    odd = [[hop(x, 1, 1)] for x in (low, high)]
    odd[0][0], _ = lax.optimization_barrier((odd[0][0], even[0][0]))
    for chains, side in ((even, 0), (odd, 1)):
        for chain in chains:
            for step in range(2, col_count):
                x = hop(chain[-1], side, step)
                if x is not None:
                    chain.append(x)
    split_chain, other_chain = list(zip(*even)), list(zip(*odd))
    n_ids, n_goals = (-(-n // META) * META for n in (row_count, 2 * col_count))
    one = swap(r_pay, "row", 2)
    r_later, *rest = lax.optimization_barrier((r_pay, other_chain[1][0]))
    other_chain[1] = (rest[0], other_chain[1][1])
    chips = [r_pay, one] + [swap(r_later, "row", m) for m in range(4, row_count, 2)]
    chips, *rest = lax.optimization_barrier((chips, other_chain[1][1]))
    other_chain[1] = (other_chain[1][0], rest[0])
    panel_pays = [x for pair in zip(chips, [swap(x, "row", 1) for x in chips]) for x in pair]

    def stage(first, last, n_prev, state, pays):
        out = [
            shape(fine_rows * coarse_cols, tile, 2 * tile),
            shape(fine_rows, col_count * tile, 2 * tile, dtype=bf16),
            shape(n_goals, 2 * tile),
        ]
        scratch = [
            pltpu.SMEM((n_ids, 2 * tile), f32),
            pltpu.SMEM((len(pays), META, 2 * tile), f32),
            pltpu.SMEM((n_goals, 2 * tile), f32),
            pltpu.SemaphoreType.DMA((len(pays) + 2,)),
        ]
        if first:
            out += [shape(fine_total + 1, tile, 2 * tile, dtype=bf16), shape(n_ids, 2 * tile)]
        if last:
            spread = n_chips * owned
            scratch = [
                pltpu.VMEM(out[0].shape, f32),
                pltpu.VMEM(out[1].shape, bf16),
                pltpu.VMEM((2 * spread + 1, tile, coarse_cols * tile), f32),
                pltpu.SMEM((col_count, fine_rows), i32),
            ] + scratch
            out = [shape(fine_rows, tile, coarse_cols * tile)] + [shape(spread, tile, coarse_cols * tile)] * 2
        operands = list(state) + [x for pay in pays for x in pay]
        kernel = functools.partial(products, first, last, row_count, n_prev, len(pays), sizes)
        return call(kernel, tuple(out), len(operands), scratch, flops=2**28, nbytes=4 * 2**20)(*operands)

    early = [(low, high)] + split_chain[:1] + other_chain[:1]
    middle = split_chain[1:-1] + other_chain[1:]
    late = split_chain[-1:]
    acc, weights, goals, panel, ids = stage(True, False, 0, panel_pays, early + middle)
    strips, keep, send = stage(False, True, len(early + middle), (acc, panel, weights, ids, goals), late)

    received = swap(send, "row", 1)
    product = call(
        write_product, shape(fine_rows, coarse_cols, tile, tile), 1, flops=2**24, nbytes=2**20
    )(strips)
    part = shape(owned, tile, coarse_cols * tile)
    parts = call(add_pair, (part,) * n_chips, 2, nbytes=2**20)(keep, received)
    others = [swap(parts[m], "row", 2 * m) for m in range(1, n_chips)]
    coarse = call(add_all, shape(owned, coarse_cols, tile, tile), n_chips, nbytes=2**20)(parts[0], *others)
    return (product, coarse)


def solution(mesh):
    return jax.shard_map(
        shards,
        mesh=mesh,
        in_specs=(
            P("row", "col", None, None),
            P("row", "col"),
            P("row", "col"),
            P("row", "col"),
            P("row", "col", None, None),
            P("row", "col"),
            P("row", "col"),
        ),
        out_specs=(P("row", "col", None, None), P("row", "col", None, None)),
        check_vma=False,
    )
```
